128 devices in a mesh: pix: 16 (over z, x_lo, core), img: 8 (over x_hi, y).
Axes of the slice: x: 4 (x_hi: 2, x_lo: 2; x = x_hi * 2 + x_lo), y: 4, z: 4, core: 2. Of those that a mesh axis runs over, the one named last changes fastest.
Arguments:
- images: bfloat16 [16384, 16384], P('img', 'pix'), may hold values from -6 to 6
- signs: int32 [16384], P('pix'), may hold values from -1 to 1, as said below
- kept: int32 [512], replicated, may hold values from 0 to 16383, as said below
- omega: bfloat16 [16384, 256], P('img'), may hold values from -0.0625 to 0.0625
Outputs:
- sketch: float32 [256, 512], P('img', 'pix')
The draws below stay inside these ranges and needn't reach their ends.
Inputs may be any that keep to these rules, and one draw needn't show every extreme that they name: signs are -1 or +1. `kept`: the indices are distinct.
All inputs are finite; a program needn't handle non-finite values.
Results may differ from the reference program's by a relative error of at most 0.0003.
Values sent between devices are 32-bit elements; how exact they have to be, the bound alone decides.
A program may use at most 64 MiB of HBM per device.

```python
import jax
import jax.numpy as jnp
from jax import lax

NPIX = 16384
KEEP = 512
RANK = 256
IMG_DEV = 2048
IMAGES = 16384
N_IMG = 8


def draw_signs(key, part):
    key = jax.random.fold_in(key, 1)
    return (2 * jax.random.randint(key, (NPIX,), 0, 2) - 1).astype(jnp.int32)


def draw_kept(key, part):
    key = jax.random.fold_in(key, 2)
    return jax.random.permutation(key, NPIX)[:KEEP].astype(jnp.int32)


def raised(values, stream_key, source, target, blocks, factor):
    owner, partner = [(jnp.arange(values.shape[dim]) // (values.shape[dim] // blocks)).reshape([-1 if axis == dim else 1 for axis in range(values.ndim)]) for dim in (source, target)]
    chosen = jax.random.permutation(stream_key, blocks)[partner]
    strong = (owner == chosen) | (owner == (partner + blocks // 2) % blocks)
    return jnp.where(strong, factor * values, values)


def levels(rng, extent, split, low, top_value):
    gain, own = 1.0, jax.random.fold_in(rng, 6)
    for axis_at, blocks in split:
        heights = jnp.exp(jax.random.uniform(jax.random.fold_in(own, axis_at), (blocks,), jnp.float32, low / len(split), top_value / len(split)))
        gain = gain * jnp.repeat(heights, extent[axis_at] // blocks).reshape([-1 if axis == axis_at else 1 for axis in range(len(extent))])
    return gain


def scatter_about(rng, extent, width, limit, cuts=(), kind=jnp.bfloat16):
    drawn = width * jax.random.normal(rng, extent, jnp.float32)
    if cuts:
        drawn = drawn * levels(rng, extent, cuts, -0.22, 0.18)
    return jnp.clip(drawn, -limit, limit).astype(kind)


def gaussian_with(rng, shape, deviation, reach, cuts, heavy, held_as=jnp.bfloat16):
    drawn = deviation * jax.random.normal(rng, shape, jnp.float32)
    if cuts:
        drawn = drawn * levels(rng, shape, cuts, -0.22, 0.18)
    return jnp.clip(raised(drawn, jax.random.fold_in(rng, 3), *heavy), -reach, reach).astype(held_as)


def setup_inputs(seed: int = 0) -> dict:
    splits = jax.random.split(jax.random.key(seed), 5)
    return {
        "images": scatter_about(splits[0], (IMAGES, NPIX), 1.0, 6.0, ((0, 8), (1, 16))),
        "signs": draw_signs(jax.random.fold_in(splits[4], 71), 0),
        "kept": draw_kept(jax.random.fold_in(splits[4], 71), 0),
        "omega": gaussian_with(splits[3], (IMAGES, RANK), IMAGES ** -0.5, 0.0625, ((0, 8),), (0, 1, 8, 2.0)),
    }


def walsh(values):
    rows = values.shape[0]
    count = values.shape[1]
    for section in range(count.bit_length() - 1):
        half = 1 << section
        shaped = values.reshape(rows, -1, 2, half)
        lower = shaped[:, :, 0]
        upper = shaped[:, :, 1]
        values = jnp.stack([lower + upper, lower - upper], axis=2).reshape(rows, count)
    return values

def reference(images, signs, kept, omega):
    sign_row = signs.astype(jnp.bfloat16)[None, :]
    columns = kept.astype(jnp.int32)

    def accumulate(total, pair):
        block, weights = pair
        signed = block * sign_row
        coeffs = walsh(signed.astype(jnp.float32)) * float(NPIX) ** (-0.5)
        picked = jnp.take(coeffs, columns, axis=1)
        robust = picked / jnp.sqrt(1.0 + picked * picked)
        term = jnp.dot(weights.astype(jnp.float32).T, robust, precision=lax.Precision.HIGHEST)
        return (total + term, None)
    start = jnp.zeros((RANK, KEEP), jnp.float32)
    sketch, _ = lax.scan(accumulate, start, (images.reshape(N_IMG, IMG_DEV, NPIX), omega.reshape(N_IMG, IMG_DEV, RANK)))
    return sketch
```

```python
import jax
import jax.numpy as jnp
from jax import lax
from jax.sharding import PartitionSpec as P

NPIX = 16384


def hadamard_rows(columns, base, width):
    pixel = base + lax.iota(jnp.int32, width)
    common = columns[:, None] & pixel[None, :]
    return (1 - 2 * (lax.population_count(common) & 1)).astype(jnp.bfloat16)


def local(images, signs, kept, omega):
    width = images.shape[1]
    place = lax.axis_index("pix")
    rows = hadamard_rows(kept, place * width, width) * signs.astype(jnp.bfloat16)[None, :]
    partial = lax.dot_general(rows, images, (((1,), (1,)), ((), ())), preferred_element_type=jnp.float32)
    picked = lax.psum_scatter(partial, "pix", scatter_dimension=0, tiled=True) * float(NPIX) ** (-0.5)
    robust = picked * lax.rsqrt(1.0 + picked * picked)
    sketch = lax.dot_general(
        omega.astype(jnp.float32), robust, (((0,), (1,)), ((), ())), precision=lax.Precision.HIGHEST
    )
    return lax.psum_scatter(sketch, "img", scatter_dimension=0, tiled=True)


def solution(mesh):
    in_specs = (P("img", "pix"), P("pix"), P(), P("img", None))
    out_specs = P("img", "pix")
    return jax.shard_map(local, mesh=mesh, in_specs=in_specs, out_specs=out_specs, check_vma=False)
```

```python
import functools

import jax
import jax.numpy as jnp
from jax import lax
from jax.experimental import pallas as pl
from jax.experimental.pallas import tpu as pltpu
from jax.sharding import PartitionSpec as P

NPIX = 16384
MESH = pl.DeviceIdType.MESH
KINDS = "BABBABAB"
COUNT = len(KINDS)
LAG = 2
PIECES = ((1, 1), (2, 0), (2, 1), (3, 0), (1, 0), (3, 1), (0, 0), (0, 1))


def transfer(src, dst, send, recv, peer):
    return pltpu.make_async_remote_copy(
        src_ref=src, dst_ref=dst, send_sem=send, recv_sem=recv, device_id=peer, device_id_type=MESH
    )


def kernel(tasks, images, signs_far, kept_far, omega, out, signs, kept, pixels, weights, hada, column, part, fromcore, fromx, z_first, z_second,
           total, slabs, load_sem, send_sem, recv_sem, slab_send, slab_recv):
    place, slab = lax.axis_index("pix"), lax.axis_index("img")
    width = images.shape[1]
    chunk = images.shape[0] // COUNT
    z, x, core = place // 4, place // 2 % 2, place % 2
    sibling = {"pix": z * 4 + x * 2 + (1 - core)}
    across = {"pix": z * 4 + (1 - x) * 2 + core}
    above = {"pix": (z + 1) % 4 * 4 + x * 2 + core}
    below = {"pix": (z + 3) % 4 * 4 + x * 2 + core}
    others = [{"img": (slab + step) % 8} for step in range(1, 8)]

    loads = [
        pltpu.make_async_copy(images.at[pl.ds(i * chunk, chunk)], pixels.at[i], load_sem.at[i]) for i in range(COUNT)
    ]
    loads.append(pltpu.make_async_copy(omega, weights, load_sem.at[COUNT]))
    small = [
        pltpu.make_async_copy(kept_far, kept, load_sem.at[COUNT + 1]),
        pltpu.make_async_copy(signs_far, signs, load_sem.at[COUNT + 2]),
    ]
    for load in small + loads:
        load.start()
    barrier = pltpu.get_barrier_semaphore()
    for peer in [sibling, across, above, below] + others:
        pl.semaphore_signal(barrier, inc=1, device_id=peer, device_id_type=MESH)

    for load in small:
        load.wait()
    for i in range(4):
        row = kept[pl.ds(i * 128, 128)].reshape(1, 128)
        column[i * 128:(i + 1) * 128, :] = jnp.broadcast_to(row, (128, 128)).T
    lane = lax.broadcasted_iota(jnp.int32, (32, 128), 1)
    marks = [signs[pl.ds(j * 128, 128)].reshape(1, 128).astype(jnp.float32) for j in range(width // 128)]

    def sign_of(bits):
        return (1 - 2 * (lax.population_count(bits) & 1)).astype(jnp.float32)

    for rc in range(2):
        for rx in range(2):
            for rz in range(4):
                owner = (z + rz) % 4 * 4 + (x + rx) % 2 * 2 + (core + rc) % 2
                index = column[pl.ds(pl.multiple_of(owner * 32, 32), 32), :]
                low = sign_of(index & (lane + place * width))
                flips = [(1 - 2 * (index >> b & 1)).astype(jnp.float32) for b in (7, 8, 9)]
                halves = [(rc * 2 + rx) * 128 + PIECES.index((rz, half)) * 16 for half in range(2)]
                for j in range(width // 128):
                    value = low * marks[j]
                    for b in range(3):
                        if j >> b & 1:
                            value = value * flips[b]
                    value = value.astype(jnp.bfloat16)
                    for half in range(2):
                        hada[halves[half]:halves[half] + 16, j * 128:(j + 1) * 128] = value[half * 16:half * 16 + 16]

    sends = {}
    used = iter(range(1000))

    def start(key, src, dst, peer):
        at = next(used)
        copy = transfer(src, dst, send_sem.at[at], recv_sem.at[at], peer)
        copy.start()
        sends[key] = copy

    def kinds(i):
        return slice(0, 1) if KINDS[i] == "A" else slice(0, 2)

    def multiply(i, rc):
        value = lax.dot_general(
            hada[rc * 256:(rc + 1) * 256, :], pixels[i], (((1,), (1,)), ((), ())), preferred_element_type=jnp.float32
        )
        part[i, rc] = value.reshape(2, 8, 16, chunk)

    def first_round(i):
        rx = kinds(i)
        start(("up", i), part.at[i, 0, rx, 0:2], z_first.at[i, 0, rx], above)
        start(("down", i), part.at[i, 0, rx, 2:4], z_first.at[i, 1, rx], below)

    def core_done(i):
        sends["core", i].wait_recv()
        part[i, 0] = part[i, 0] + fromcore[i]
        if KINDS[i] == "A":
            start(("x", i), part.at[i, 0, 1], fromx.at[i], across)
        else:
            first_round(i)

    def x_done(i):
        sends["x", i].wait_recv()
        part[i, 0, 0] = part[i, 0, 0] + fromx[i]
        first_round(i)

    def first_done(i):
        rx = kinds(i)
        sends["up", i].wait_recv()
        part[i, 0, rx, 4] = part[i, 0, rx, 4] + z_first[i, 0, rx, 1]
        start(("up2", i), part.at[i, 0, rx, 4], z_second.at[i, 0, rx], above)
        sends["down", i].wait_recv()
        part[i, 0, rx, 5] = part[i, 0, rx, 5] + z_first[i, 1, rx, 0]
        start(("down2", i), part.at[i, 0, rx, 5], z_second.at[i, 1, rx], below)

    def ring_sum(i, rx):
        upper = part[i, 0, rx, 6] + z_first[i, 1, rx, 1] + z_second[i, 0, rx]
        lower = part[i, 0, rx, 7] + z_first[i, 0, rx, 0] + z_second[i, 1, rx]
        return upper, lower

    def second_done(i):
        sends["up2", i].wait_recv()
        sends["down2", i].wait_recv()
        if KINDS[i] == "A":
            finish(i, ring_sum(i, 0))
        else:
            upper, lower = ring_sum(i, 1)
            part[i, 0, 1, 6] = upper
            part[i, 0, 1, 7] = lower
            start(("late", i), part.at[i, 0, 1, 6:8], fromx.at[i, 0:2], across)

    def late_done(i):
        sends["late", i].wait_recv()
        upper, lower = ring_sum(i, 0)
        finish(i, (upper + fromx[i, 0], lower + fromx[i, 1]))

    def finish(i, halves):
        picked = jnp.concatenate(halves, axis=0) * float(NPIX) ** (-0.5)
        robust = picked * lax.rsqrt(1.0 + picked * picked)
        high = robust.astype(jnp.bfloat16)
        rest = (robust - high.astype(jnp.float32)).astype(jnp.bfloat16)
        both = jnp.concatenate([high, rest], axis=0)
        term = jnp.dot(both, weights[pl.ds(i * chunk, chunk), :], preferred_element_type=jnp.float32)
        sketch.append(term[:32] + term[32:])

    sketch = []
    for i in range(COUNT):
        loads[i].wait()
        multiply(i, 1)
        if i == 0:
            pl.semaphore_wait(barrier, 4 + len(others))
        start(("core", i), part.at[i, 1], fromcore.at[i], sibling)
        multiply(i, 0)
        if i >= LAG:
            core_done(i - LAG)
    for i in range(COUNT - LAG, COUNT):
        core_done(i)
    loads[COUNT].wait()
    steps = dict(x=x_done, f=first_done, s=second_done, l=late_done)
    for name, i in tasks:
        steps[name](i)

    whole = functools.reduce(lambda a, b: a + b, sketch)
    total[0] = whole[:, :128]
    total[1] = whole[:, 128:]
    final = []
    for step, peer in enumerate(others):
        copy = transfer(total.at[peer["img"] // 4], slabs.at[step], slab_send.at[step], slab_recv.at[step], peer)
        copy.start()
        final.append(copy)
    for copy in sends.values():
        copy.wait_send()
    result = total[slab // 4]
    for step, copy in enumerate(final):
        copy.wait_recv()
        result = result + slabs[step]
    turned = jnp.concatenate([result, jnp.zeros((96, 128), jnp.float32)], axis=0).T
    column_block = [turned[32 * n:32 * n + 32, 0:32] for n in range(4)]
    mine = column_block[0]
    for n in range(1, 4):
        mine = jnp.where(slab % 4 == n, column_block[n], mine)
    out[...] = mine
    for copy in final:
        copy.wait_send()


def default_tasks():
    tasks = []
    for i in range(COUNT):
        if KINDS[i] == "B":
            tasks.append(("f", i))
        else:
            tasks.append(("x", i))
    for i in range(COUNT):
        if KINDS[i] == "B":
            tasks.append(("s", i))
        else:
            tasks.append(("f", i))
    for i in range(COUNT):
        if KINDS[i] == "B":
            tasks.append(("l", i))
        else:
            tasks.append(("s", i))
    return tasks


def local(images, signs, kept, omega):
    rows, width = images.shape
    chunk = rows // COUNT
    copies = 6 * COUNT
    return pl.pallas_call(
        functools.partial(kernel, default_tasks()),
        out_shape=jax.ShapeDtypeStruct((32, 32), jnp.float32),
        in_specs=[
            pl.BlockSpec(memory_space=pltpu.HBM),
            pl.BlockSpec(memory_space=pltpu.HBM),
            pl.BlockSpec(memory_space=pltpu.HBM),
            pl.BlockSpec(memory_space=pltpu.HBM),
        ],
        out_specs=pl.BlockSpec(memory_space=pltpu.VMEM),
        scratch_shapes=[
            pltpu.VMEM(signs.shape, jnp.int32),
            pltpu.VMEM(kept.shape, jnp.int32),
            pltpu.VMEM((COUNT, chunk, width), jnp.bfloat16),
            pltpu.VMEM(omega.shape, jnp.bfloat16),
            pltpu.VMEM((512, width), jnp.bfloat16),
            pltpu.VMEM((512, 128), jnp.int32),
            pltpu.VMEM((COUNT, 2, 2, 8, 16, chunk), jnp.float32),
            pltpu.VMEM((COUNT, 2, 8, 16, chunk), jnp.float32),
            pltpu.VMEM((COUNT, 8, 16, chunk), jnp.float32),
            pltpu.VMEM((COUNT, 2, 2, 2, 16, chunk), jnp.float32),
            pltpu.VMEM((COUNT, 2, 2, 16, chunk), jnp.float32),
            pltpu.VMEM((2, 32, 128), jnp.float32),
            pltpu.VMEM((7, 32, 128), jnp.float32),
            pltpu.SemaphoreType.DMA((COUNT + 3,)),
            pltpu.SemaphoreType.DMA((copies,)),
            pltpu.SemaphoreType.DMA((copies,)),
            pltpu.SemaphoreType.DMA((7,)),
            pltpu.SemaphoreType.DMA((7,)),
        ],
        compiler_params=pltpu.CompilerParams(collective_id=0, has_side_effects=True, vmem_limit_bytes=64 << 20),
        cost_estimate=pl.CostEstimate(flops=2 * rows * width * 512, bytes_accessed=5 << 20, transcendentals=0),
        name="sketch",
    )(images, signs, kept, omega)


def solution(mesh):
    in_specs = (P("img", "pix"), P("pix"), P(), P("img", None))
    out_specs = P("img", "pix")
    return jax.shard_map(local, mesh=mesh, in_specs=in_specs, out_specs=out_specs, check_vma=False)
```

```python
import functools

import jax
import jax.numpy as jnp
from jax import lax
from jax.experimental import pallas as pl
from jax.experimental.pallas import tpu as pltpu
from jax.sharding import PartitionSpec as P

NPIX = 16384
MESH = pl.DeviceIdType.MESH
CHUNKS = (
    ("B", 128), ("A", 128), ("B", 256), ("A", 256), ("B", 256), ("A", 256), ("B", 256), ("A", 256), ("B", 256),
)
COUNT = len(CHUNKS)
STARTS = [sum(size for _, size in CHUNKS[:i]) for i in range(COUNT)]
GROUPS = ((0, 2), (2, 2), (4, 2), (6, 3))
ORDER = (
    ("m", 0), ("m", 1), ("c", 0), ("c", 1), ("m", 2), ("c", 2), ("c", 3), ("m", 3), ("c", 4), ("f", 0),
    ("c", 5), ("x", 1), ("c", 6), ("c", 7), ("f", 2), ("c", 8), ("f", 4), ("x", 3), ("s", 0), ("f", 1),
    ("f", 6), ("s", 2), ("x", 5), ("f", 8), ("s", 4), ("x", 7), ("f", 3), ("s", 1), ("l", 0), ("s", 6),
    ("l", 2), ("f", 5), ("l", 4), ("s", 8), ("f", 7), ("s", 3), ("l", 6), ("s", 5), ("l", 8), ("s", 7),
)
PIECES = ((1, 1), (2, 0), (2, 1), (3, 0), (1, 0), (3, 1), (0, 0), (0, 1))


def transfer(src, dst, send, recv, peer):
    return pltpu.make_async_remote_copy(
        src_ref=src, dst_ref=dst, send_sem=send, recv_sem=recv, device_id=peer, device_id_type=MESH
    )


def kernel(images, signs_far, kept_far, omega, out, signs, kept, pixels, weights, hada, column, total, packed, slabs,
           load_sem, send_sem, recv_sem, slab_send, slab_recv, near, far, *buffers):
    part, fromcore, fromx, z_first, z_second = (buffers[n * COUNT:(n + 1) * COUNT] for n in range(5))
    place, slab = lax.axis_index("pix"), lax.axis_index("img")
    width = images.shape[1]
    z, x, core = place // 4, place // 2 % 2, place % 2
    sibling = {"pix": z * 4 + x * 2 + (1 - core)}
    across = {"pix": z * 4 + (1 - x) * 2 + core}
    above = {"pix": (z + 1) % 4 * 4 + x * 2 + core}
    below = {"pix": (z + 3) % 4 * 4 + x * 2 + core}
    others = [{"img": (slab + step) % 8} for step in range(1, 8)]

    loads = []
    for i, (_, size) in enumerate(CHUNKS):
        here = pl.ds(STARTS[i], size)
        loads.append(pltpu.make_async_copy(images.at[here], pixels.at[here], load_sem.at[i]))
    loads.append(pltpu.make_async_copy(omega, weights, load_sem.at[COUNT]))
    small = [
        pltpu.make_async_copy(kept_far, kept, load_sem.at[COUNT + 1]),
        pltpu.make_async_copy(signs_far, signs, load_sem.at[COUNT + 2]),
    ]
    for load in small + loads:
        load.start()
    barrier = pltpu.get_barrier_semaphore()
    beside = [{"img": slab // 4 * 4 + (slab + step) % 4} for step in (1, 3)] + [{"img": (slab + 4) % 8}]
    greeted = [sibling, across, above, below] + beside
    for peer in greeted:
        pl.semaphore_signal(barrier, inc=1, device_id=peer, device_id_type=MESH)

    def tell(known):
        for peer in beside:
            pl.semaphore_signal(known, inc=1, device_id=peer, device_id_type=MESH)

    def hear(known):
        pl.semaphore_wait(known, len(beside))

    for load in small:
        load.wait()
    for i in range(4):
        row = kept[pl.ds(i * 128, 128)].reshape(1, 128)
        column[i * 128:(i + 1) * 128, :] = jnp.broadcast_to(row, (128, 128)).T
    lane = lax.broadcasted_iota(jnp.int32, (32, 128), 1)
    marks = [signs[pl.ds(j * 128, 128)].reshape(1, 128).astype(jnp.float32) for j in range(width // 128)]

    def sign_of(bits):
        return (1 - 2 * (lax.population_count(bits) & 1)).astype(jnp.float32)

    for rc in (1, 0):
        for rx in range(2):
            for rz in range(4):
                owner = (z + rz) % 4 * 4 + (x + rx) % 2 * 2 + (core + rc) % 2
                index = column[pl.ds(pl.multiple_of(owner * 32, 32), 32), :]
                low = sign_of(index & (lane + place * width))
                flips = [(1 - 2 * (index >> b & 1)).astype(jnp.float32) for b in (7, 8, 9)]
                halves = [(rc * 2 + rx) * 128 + PIECES.index((rz, half)) * 16 for half in range(2)]
                for j in range(width // 128):
                    value = low * marks[j]
                    for b in range(3):
                        if j >> b & 1:
                            value = value * flips[b]
                    value = value.astype(jnp.bfloat16)
                    for half in range(2):
                        hada[halves[half]:halves[half] + 16, j * 128:(j + 1) * 128] = value[half * 16:half * 16 + 16]

    sends = {}

    def start(key, src, dst, peer):
        at = len(sends)
        copy = transfer(src, dst, send_sem.at[at], recv_sem.at[at], peer)
        copy.start()
        sends[key] = copy

    def lines(i):
        return slice(0, 1) if CHUNKS[i][0] == "A" else slice(0, 2)

    def matmul(group):
        first, count = GROUPS[group]
        size = sum(CHUNKS[i][1] for i in range(first, first + count))
        for i in range(first, first + count):
            loads[i].wait()
        value = lax.dot_general(
            hada[...], pixels[pl.ds(STARTS[first], size), :], (((1,), (1,)), ((), ())), preferred_element_type=jnp.float32
        )
        for i in range(first, first + count):
            at = STARTS[i] - STARTS[first]
            part[i][...] = value[:, at:at + CHUNKS[i][1]].reshape(part[i].shape)
        if first == 0:
            pl.semaphore_wait(barrier, len(greeted))
        for i in range(first, first + count):
            start(("core", i), part[i].at[1], fromcore[i], sibling)

    def first_round(i):
        rx = lines(i)
        start(("up", i), part[i].at[0, rx, 0:2], z_first[i].at[0], above)
        start(("down", i), part[i].at[0, rx, 2:4], z_first[i].at[1], below)

    def core_done(i):
        sends["core", i].wait_recv()
        if CHUNKS[i][0] == "A":
            part[i][0, 1] = part[i][0, 1] + fromcore[i][1]
            start(("x", i), part[i].at[0, 1], fromx[i], across)
            part[i][0, 0] = part[i][0, 0] + fromcore[i][0]
        else:
            part[i][0, :, 0:4] = part[i][0, :, 0:4] + fromcore[i][:, 0:4]
            first_round(i)
            part[i][0, :, 4:8] = part[i][0, :, 4:8] + fromcore[i][:, 4:8]

    def x_done(i):
        sends["x", i].wait_recv()
        part[i][0, 0, 0:4] = part[i][0, 0, 0:4] + fromx[i][0:4]
        first_round(i)
        part[i][0, 0, 4:8] = part[i][0, 0, 4:8] + fromx[i][4:8]

    def first_done(i):
        rx = lines(i)
        sends["up", i].wait_recv()
        part[i][0, rx, 4] = part[i][0, rx, 4] + z_first[i][0, :, 1]
        start(("up2", i), part[i].at[0, rx, 4], z_second[i].at[0], above)
        sends["down", i].wait_recv()
        part[i][0, rx, 5] = part[i][0, rx, 5] + z_first[i][1, :, 0]
        start(("down2", i), part[i].at[0, rx, 5], z_second[i].at[1], below)

    def ring_sum(i, rx):
        upper = part[i][0, rx, 6] + z_first[i][1, rx, 1] + z_second[i][0, rx]
        lower = part[i][0, rx, 7] + z_first[i][0, rx, 0] + z_second[i][1, rx]
        return upper, lower

    def second_done(i):
        sends["up2", i].wait_recv()
        sends["down2", i].wait_recv()
        if CHUNKS[i][0] == "A":
            finish(i, ring_sum(i, 0))
        else:
            upper, lower = ring_sum(i, 1)
            part[i][0, 1, 6] = upper
            part[i][0, 1, 7] = lower
            start(("late", i), part[i].at[0, 1, 6:8], fromx[i], across)
            upper, lower = ring_sum(i, 0)
            part[i][0, 0, 6] = upper
            part[i][0, 0, 7] = lower

    def late_done(i):
        sends["late", i].wait_recv()
        finish(i, (part[i][0, 0, 6] + fromx[i][0], part[i][0, 0, 7] + fromx[i][1]))

    finished = []

    def finish(i, halves):
        picked = jnp.concatenate(halves, axis=0) * float(NPIX) ** (-0.5)
        robust = picked * lax.rsqrt(1.0 + picked * picked)
        high = robust.astype(jnp.bfloat16)
        rest = (robust - high.astype(jnp.float32)).astype(jnp.bfloat16)
        both = jnp.concatenate([high, rest], axis=0)
        if not finished:
            loads[COUNT].wait()
        term = jnp.dot(both, weights[pl.ds(STARTS[i], CHUNKS[i][1]), :], preferred_element_type=jnp.float32)
        term = term[:32] + term[32:]
        for n in range(2):
            fresh = term[:, n * 128:(n + 1) * 128]
            total[n] = total[n] + fresh if finished else fresh
        finished.append(i)

    steps = dict(m=matmul, c=core_done, x=x_done, f=first_done, s=second_done, l=late_done)
    for at, (name, i) in enumerate(ORDER):
        steps[name](i)
        if at == len(ORDER) // 4:
            tell(near)
        if at == len(ORDER) // 2:
            hear(near)
            tell(far)
    hear(far)

    for n in range(8):
        lanes = slice(n % 4 * 32, n % 4 * 32 + 32)
        packed[n] = jnp.concatenate([total[n // 4, 8 * q:8 * q + 8, lanes] for q in range(4)], axis=1)
    final = []
    for step, peer in enumerate(others):
        copy = transfer(packed.at[peer["img"]], slabs.at[step], slab_send.at[step], slab_recv.at[step], peer)
        copy.start()
        final.append(copy)
    for copy in sends.values():
        copy.wait_send()
    result = packed[slab]
    for step, copy in enumerate(final):
        copy.wait_recv()
        result = result + slabs[step]
    block = jnp.concatenate([result[:, 32 * q:32 * q + 32] for q in range(4)], axis=0)
    out[...] = block.T
    for copy in final:
        copy.wait_send()


def local(images, signs, kept, omega):
    rows, width = images.shape
    copies = 6 * COUNT
    scratch = [
        pltpu.VMEM(signs.shape, jnp.int32),
        pltpu.VMEM(kept.shape, jnp.int32),
        pltpu.VMEM((rows, width), jnp.bfloat16),
        pltpu.VMEM(omega.shape, jnp.bfloat16),
        pltpu.VMEM((512, width), jnp.bfloat16),
        pltpu.VMEM((512, 128), jnp.int32),
        pltpu.VMEM((2, 32, 128), jnp.float32),
        pltpu.VMEM((8, 8, 128), jnp.float32),
        pltpu.VMEM((7, 8, 128), jnp.float32),
        pltpu.SemaphoreType.DMA((COUNT + 3,)),
        pltpu.SemaphoreType.DMA((copies,)),
        pltpu.SemaphoreType.DMA((copies,)),
        pltpu.SemaphoreType.DMA((7,)),
        pltpu.SemaphoreType.DMA((7,)),
        pltpu.SemaphoreType.REGULAR,
        pltpu.SemaphoreType.REGULAR,
    ]
    lines = [1 if kind == "A" else 2 for kind, _ in CHUNKS]
    scratch += [pltpu.VMEM((2, 2, 8, 16, size), jnp.float32) for _, size in CHUNKS]
    scratch += [pltpu.VMEM((2, 8, 16, size), jnp.float32) for _, size in CHUNKS]
    scratch += [pltpu.VMEM((8 if kind == "A" else 2, 16, size), jnp.float32) for kind, size in CHUNKS]
    scratch += [pltpu.VMEM((2, n, 2, 16, size), jnp.float32) for n, (_, size) in zip(lines, CHUNKS)]
    scratch += [pltpu.VMEM((2, n, 16, size), jnp.float32) for n, (_, size) in zip(lines, CHUNKS)]
    return pl.pallas_call(
        kernel,
        out_shape=jax.ShapeDtypeStruct((32, 32), jnp.float32),
        in_specs=[pl.BlockSpec(memory_space=pl.ANY)] * 4,
        out_specs=pl.BlockSpec(memory_space=pltpu.VMEM),
        scratch_shapes=scratch,
        compiler_params=pltpu.CompilerParams(collective_id=0, has_side_effects=True, vmem_limit_bytes=48 << 20),
        cost_estimate=pl.CostEstimate(flops=2 * rows * width * 512, bytes_accessed=5 << 20, transcendentals=0),
        name="sketch",
    )(*(pltpu.with_memory_space_constraint(array, pltpu.HBM) for array in (images, signs, kept, omega)))


def solution(mesh):
    in_specs = (P("img", "pix"), P("pix"), P(), P("img", None))
    out_specs = P("img", "pix")
    return jax.shard_map(local, mesh=mesh, in_specs=in_specs, out_specs=out_specs, check_vma=False)
```

```python
import functools

import jax
import jax.numpy as jnp
from jax import lax
from jax.experimental import pallas as pl
from jax.experimental.pallas import tpu as pltpu
from jax.sharding import PartitionSpec as P

NPIX = 16384
MESH = pl.DeviceIdType.MESH
CHUNKS = (
    ("B", 256), ("B", 256), ("A", 256), ("B", 384), ("A", 128), ("A", 256), ("B", 128), ("B", 256), ("A", 128),
)
COUNT = len(CHUNKS)
STARTS = [sum(size for _, size in CHUNKS[:i]) for i in range(COUNT)]
GROUPS = ((0, 1), (1, 2), (3, 2), (5, 2), (7, 1), (8, 1))
ORDER = (
    ("m", 0), ("m", 1), ("c", 0), ("m", 2), ("c", 1), ("c", 2), ("m", 3), ("c", 3), ("c", 4), ("m", 4),
    ("c", 5), ("c", 6), ("m", 5), ("c", 7), ("c", 8), ("f", 0), ("f", 1), ("x", 2), ("f", 3), ("x", 4),
    ("f", 6), ("f", 7), ("x", 5), ("s", 0), ("s", 1), ("x", 8), ("f", 2), ("s", 3), ("f", 4), ("l", 0),
    ("s", 6), ("l", 1), ("s", 7), ("f", 5), ("f", 8), ("s", 2), ("s", 4), ("l", 3), ("l", 6), ("l", 7),
    ("s", 5), ("s", 8),
)
PIECES = ((1, 1), (2, 0), (2, 1), (3, 0), (1, 0), (3, 1), (0, 0), (0, 1))


def transfer(src, dst, send, recv, peer):
    return pltpu.make_async_remote_copy(
        src_ref=src, dst_ref=dst, send_sem=send, recv_sem=recv, device_id=peer, device_id_type=MESH
    )


def kernel(images, signs_far, kept_far, omega, out, signs, kept, pixels, weights, hada, column, total, packed, slabs,
           load_sem, small_sem, send_sem, own_sem, x_sem, first_sem, slab_send, slab_recv, near, far, *buffers):
    part, fromcore, fromx, z_first, z_second = (buffers[n * COUNT:(n + 1) * COUNT] for n in range(5))
    place, slab = lax.axis_index("pix"), lax.axis_index("img")
    width = images.shape[1]
    z, x, core = place // 4, place // 2 % 2, place % 2
    sibling = {"pix": z * 4 + x * 2 + (1 - core)}
    across = {"pix": z * 4 + (1 - x) * 2 + core}
    above = {"pix": (z + 1) % 4 * 4 + x * 2 + core}
    below = {"pix": (z + 3) % 4 * 4 + x * 2 + core}
    others = [{"img": (slab + step) % 8} for step in range(1, 8)]

    loads = []
    for group, (first, count) in enumerate(GROUPS):
        here = pl.ds(STARTS[first], sum(CHUNKS[i][1] for i in range(first, first + count)))
        loads.append(pltpu.make_async_copy(images.at[here], pixels.at[here], load_sem.at[group]))
    small = [
        pltpu.make_async_copy(kept_far, kept, small_sem.at[0]),
        pltpu.make_async_copy(signs_far, signs, small_sem.at[1]),
    ]
    last = pltpu.make_async_copy(omega, weights, small_sem.at[0])
    for load in small + loads[:1]:
        load.start()
    barrier = pltpu.get_barrier_semaphore()
    beside = [{"img": slab // 4 * 4 + (slab + step) % 4} for step in (1, 3)] + [{"img": (slab + 4) % 8}]
    greeted = [sibling, across, above, below] + beside
    for peer in greeted:
        pl.semaphore_signal(barrier, inc=1, device_id=peer, device_id_type=MESH)

    def tell(known):
        for peer in beside:
            pl.semaphore_signal(known, inc=1, device_id=peer, device_id_type=MESH)

    def hear(known):
        pl.semaphore_wait(known, len(beside))

    for load in small:
        load.wait()
    for load in loads[1:] + [last]:
        load.start()
    for i in range(4):
        row = kept[pl.ds(i * 128, 128)].reshape(1, 128)
        column[i * 128:(i + 1) * 128, :] = jnp.broadcast_to(row, (128, 128)).T
    lane = lax.broadcasted_iota(jnp.int32, (32, 128), 1)
    marks = [signs[pl.ds(j * 128, 128)].reshape(1, 128).astype(jnp.float32) for j in range(width // 128)]

    def sign_of(bits):
        return (1 - 2 * (lax.population_count(bits) & 1)).astype(jnp.float32)

    for rc in (1, 0):
        for rx in range(2):
            for rz in range(4):
                owner = (z + rz) % 4 * 4 + (x + rx) % 2 * 2 + (core + rc) % 2
                index = column[pl.ds(pl.multiple_of(owner * 32, 32), 32), :]
                low = sign_of(index & (lane + place * width))
                flips = [(1 - 2 * (index >> b & 1)).astype(jnp.float32) for b in (7, 8, 9)]
                halves = [(rc * 2 + rx) * 128 + PIECES.index((rz, half)) * 16 for half in range(2)]
                for j in range(width // 128):
                    value = low * marks[j]
                    for b in range(3):
                        if j >> b & 1:
                            value = value * flips[b]
                    value = value.astype(jnp.bfloat16)
                    for half in range(2):
                        hada[halves[half]:halves[half] + 16, j * 128:(j + 1) * 128] = value[half * 16:half * 16 + 16]

    def start(src, dst, recv, peer):
        transfer(src, dst, send_sem, recv, peer).start()

    def arrived(dst, recv):
        transfer(dst, dst, send_sem, recv, sibling).wait_recv()

    def lines(i):
        return slice(0, 1) if CHUNKS[i][0] == "A" else slice(0, 2)

    def matmul(group):
        first, count = GROUPS[group]
        size = sum(CHUNKS[i][1] for i in range(first, first + count))
        loads[group].wait()
        value = lax.dot_general(
            hada[...], pixels[pl.ds(STARTS[first], size), :], (((1,), (1,)), ((), ())), preferred_element_type=jnp.float32
        )
        for i in range(first, first + count):
            at = STARTS[i] - STARTS[first]
            part[i][...] = value[:, at:at + CHUNKS[i][1]].reshape(part[i].shape)
        if first == 0:
            pl.semaphore_wait(barrier, len(greeted))
        for i in range(first, first + count):
            start(part[i].at[1], fromcore[i], own_sem.at[i], sibling)

    def first_round(i):
        rx = lines(i)
        start(part[i].at[0, rx, 0:2], z_first[i].at[0], first_sem.at[i], above)
        start(part[i].at[0, rx, 2:4], z_first[i].at[1], first_sem.at[i], below)

    def core_done(i):
        arrived(fromcore[i], own_sem.at[i])
        if CHUNKS[i][0] == "A":
            part[i][0, 1] = part[i][0, 1] + fromcore[i][1]
            start(part[i].at[0, 1], fromx[i], x_sem.at[i], across)
            part[i][0, 0] = part[i][0, 0] + fromcore[i][0]
        else:
            part[i][0, :, 0:4] = part[i][0, :, 0:4] + fromcore[i][:, 0:4]
            first_round(i)
            part[i][0, :, 4:8] = part[i][0, :, 4:8] + fromcore[i][:, 4:8]

    def x_done(i):
        arrived(fromx[i], x_sem.at[i])
        part[i][0, 0, 0:4] = part[i][0, 0, 0:4] + fromx[i][0:4]
        first_round(i)
        part[i][0, 0, 4:8] = part[i][0, 0, 4:8] + fromx[i][4:8]

    def first_done(i):
        rx = lines(i)
        arrived(z_first[i], first_sem.at[i])
        part[i][0, rx, 4] = part[i][0, rx, 4] + z_first[i][0, :, 1]
        start(part[i].at[0, rx, 4], z_second[i].at[0], own_sem.at[i], above)
        part[i][0, rx, 5] = part[i][0, rx, 5] + z_first[i][1, :, 0]
        start(part[i].at[0, rx, 5], z_second[i].at[1], own_sem.at[i], below)

    def ring_sum(i, rx):
        upper = part[i][0, rx, 6] + z_first[i][1, rx, 1] + z_second[i][0, rx]
        lower = part[i][0, rx, 7] + z_first[i][0, rx, 0] + z_second[i][1, rx]
        return upper, lower

    def second_done(i):
        arrived(z_second[i], own_sem.at[i])
        if CHUNKS[i][0] == "A":
            finish(i, ring_sum(i, 0))
        else:
            upper, lower = ring_sum(i, 1)
            part[i][0, 1, 6] = upper
            part[i][0, 1, 7] = lower
            start(part[i].at[0, 1, 6:8], fromx[i], x_sem.at[i], across)
            upper, lower = ring_sum(i, 0)
            part[i][0, 0, 6] = upper
            part[i][0, 0, 7] = lower

    def late_done(i):
        arrived(fromx[i], x_sem.at[i])
        finish(i, (part[i][0, 0, 6] + fromx[i][0], part[i][0, 0, 7] + fromx[i][1]))

    finished = []

    def finish(i, halves):
        picked = jnp.concatenate(halves, axis=0) * float(NPIX) ** (-0.5)
        robust = picked * lax.rsqrt(1.0 + picked * picked)
        high = robust.astype(jnp.bfloat16)
        rest = (robust - high.astype(jnp.float32)).astype(jnp.bfloat16)
        both = jnp.concatenate([high, rest], axis=0)
        if not finished:
            last.wait()
        term = jnp.dot(both, weights[pl.ds(STARTS[i], CHUNKS[i][1]), :], preferred_element_type=jnp.float32)
        term = term[:32] + term[32:]
        for n in range(2):
            fresh = term[:, n * 128:(n + 1) * 128]
            total[n] = total[n] + fresh if finished else fresh
        finished.append(i)

    steps = dict(m=matmul, c=core_done, x=x_done, f=first_done, s=second_done, l=late_done)
    for at, (name, i) in enumerate(ORDER):
        steps[name](i)
        if at == len(ORDER) // 4:
            tell(near)
        if at == len(ORDER) // 2:
            hear(near)
            tell(far)
    hear(far)

    for n in range(8):
        lanes = slice(n % 4 * 32, n % 4 * 32 + 32)
        packed[n] = jnp.concatenate([total[n // 4, 8 * q:8 * q + 8, lanes] for q in range(4)], axis=1)
    for step, peer in enumerate(others):
        transfer(packed.at[peer["img"]], slabs.at[step], slab_send, slab_recv, peer).start()
    sent = pixels.at[pl.ds(0, 480 * 4 * pixels.shape[0] // (2 * width))]
    transfer(sent, sent, send_sem, slab_recv, sibling).wait_send()
    transfer(slabs, slabs, slab_send, slab_recv, sibling).wait_recv()
    result = packed[slab]
    for step in range(len(others)):
        result = result + slabs[step]
    block = jnp.concatenate([result[:, 32 * q:32 * q + 32] for q in range(4)], axis=0)
    out[...] = block.T
    transfer(slabs, slabs, slab_send, slab_recv, sibling).wait_send()


def local(images, signs, kept, omega):
    rows, width = images.shape
    scratch = [
        pltpu.VMEM(signs.shape, jnp.int32),
        pltpu.VMEM(kept.shape, jnp.int32),
        pltpu.VMEM((rows, width), jnp.bfloat16),
        pltpu.VMEM(omega.shape, jnp.bfloat16),
        pltpu.VMEM((512, width), jnp.bfloat16),
        pltpu.VMEM((512, 128), jnp.int32),
        pltpu.VMEM((2, 32, 128), jnp.float32),
        pltpu.VMEM((8, 8, 128), jnp.float32),
        pltpu.VMEM((7, 8, 128), jnp.float32),
        pltpu.SemaphoreType.DMA((len(GROUPS),)),
        pltpu.SemaphoreType.DMA((2,)),
        pltpu.SemaphoreType.DMA,
        pltpu.SemaphoreType.DMA((COUNT,)),
        pltpu.SemaphoreType.DMA((COUNT,)),
        pltpu.SemaphoreType.DMA((COUNT,)),
        pltpu.SemaphoreType.DMA,
        pltpu.SemaphoreType.DMA,
        pltpu.SemaphoreType.REGULAR,
        pltpu.SemaphoreType.REGULAR,
    ]
    lines = [1 if kind == "A" else 2 for kind, _ in CHUNKS]
    scratch += [pltpu.VMEM((2, 2, 8, 16, size), jnp.float32) for _, size in CHUNKS]
    scratch += [pltpu.VMEM((2, 8, 16, size), jnp.float32) for _, size in CHUNKS]
    scratch += [pltpu.VMEM((8 if kind == "A" else 2, 16, size), jnp.float32) for kind, size in CHUNKS]
    scratch += [pltpu.VMEM((2, n, 2, 16, size), jnp.float32) for n, (_, size) in zip(lines, CHUNKS)]
    scratch += [pltpu.VMEM((2, n, 16, size), jnp.float32) for n, (_, size) in zip(lines, CHUNKS)]
    return pl.pallas_call(
        kernel,
        out_shape=jax.ShapeDtypeStruct((32, 32), jnp.float32),
        in_specs=[pl.BlockSpec(memory_space=pl.ANY)] * 4,
        out_specs=pl.BlockSpec(memory_space=pltpu.VMEM),
        scratch_shapes=scratch,
        compiler_params=pltpu.CompilerParams(collective_id=0, has_side_effects=True, vmem_limit_bytes=48 << 20),
        cost_estimate=pl.CostEstimate(flops=2 * rows * width * 512, bytes_accessed=5 << 20, transcendentals=0),
        name="sketch",
    )(*(pltpu.with_memory_space_constraint(array, pltpu.HBM) for array in (images, signs, kept, omega)))


def solution(mesh):
    in_specs = (P("img", "pix"), P("pix"), P(), P("img", None))
    out_specs = P("img", "pix")
    return jax.shard_map(local, mesh=mesh, in_specs=in_specs, out_specs=out_specs, check_vma=False)
```

```python
import functools

import jax
import jax.numpy as jnp
from jax import lax
from jax.experimental import pallas as pl
from jax.experimental.pallas import tpu as pltpu
from jax.sharding import PartitionSpec as P

NPIX = 16384
MESH = pl.DeviceIdType.MESH
CHUNKS = (
    ("A", 128), ("B", 256), ("A", 256), ("A", 256), ("B", 256), ("B", 256), ("B", 256), ("D", 256), ("D", 128),
)
COUNT = len(CHUNKS)
STARTS = [sum(size for _, size in CHUNKS[:i]) for i in range(COUNT)]
GROUPS = ((0, 2), (2, 2), (4, 1), (5, 2), (7, 2))
ORDER = (
    ("m", 0), ("m", 1), ("c", 0), ("c", 1), ("m", 2), ("c", 2), ("c", 3), ("m", 3), ("c", 4), ("m", 4),
    ("c", 5), ("c", 6), ("c", 7), ("c", 8), ("x", 0), ("f", 1), ("x", 2), ("f", 4), ("f", 5), ("x", 3),
    ("f", 6), ("f", 0), ("s", 1), ("f", 2), ("x", 7), ("s", 4), ("s", 5), ("x", 8), ("f", 3), ("l", 1),
    ("s", 6), ("s", 0), ("s", 2), ("l", 4), ("l", 5), ("s", 7), ("l", 6), ("s", 3), ("s", 8),
)
PIECES = ((1, 0), (1, 1), (2, 0), (2, 1), (3, 0), (3, 1), (0, 0), (0, 1))


def transfer(src, dst, send, recv, peer):
    return pltpu.make_async_remote_copy(
        src_ref=src, dst_ref=dst, send_sem=send, recv_sem=recv, device_id=peer, device_id_type=MESH
    )


def kernel(images, signs_far, kept_far, omega, out, signs, kept, pixels, weights, hada, column, total, packed, slabs,
           load_sem, small_sem, send_sem, own_sem, x_sem, first_sem, slab_send, slab_recv, near, far, *buffers):
    part, fromcore, fromx, z_first, z_second = (buffers[n * COUNT:(n + 1) * COUNT] for n in range(5))
    place, slab = lax.axis_index("pix"), lax.axis_index("img")
    width = images.shape[1]
    z, x, core = place // 4, place // 2 % 2, place % 2
    sibling = {"pix": z * 4 + x * 2 + (1 - core)}
    across = {"pix": z * 4 + (1 - x) * 2 + core}
    above = {"pix": (z + 1) % 4 * 4 + x * 2 + core}
    below = {"pix": (z + 3) % 4 * 4 + x * 2 + core}
    opposite = {"pix": (z + 2) % 4 * 4 + x * 2 + core}
    others = [{"img": (slab + step) % 8} for step in range(1, 8)]

    loads = []
    for group, (first, count) in enumerate(GROUPS):
        here = pl.ds(STARTS[first], sum(CHUNKS[i][1] for i in range(first, first + count)))
        loads.append(pltpu.make_async_copy(images.at[here], pixels.at[here], load_sem.at[group]))
    small = [
        pltpu.make_async_copy(kept_far, kept, small_sem.at[0]),
        pltpu.make_async_copy(signs_far, signs, small_sem.at[1]),
    ]
    last = pltpu.make_async_copy(omega, weights, small_sem.at[0])
    for load in small + loads[:1]:
        load.start()
    barrier = pltpu.get_barrier_semaphore()
    beside = [{"img": slab // 4 * 4 + (slab + step) % 4} for step in (1, 3)] + [{"img": (slab + 4) % 8}]
    greeted = [sibling, across, above, below] + beside
    for peer in greeted:
        pl.semaphore_signal(barrier, inc=1, device_id=peer, device_id_type=MESH)

    def tell(known):
        for peer in beside:
            pl.semaphore_signal(known, inc=1, device_id=peer, device_id_type=MESH)

    def hear(known):
        pl.semaphore_wait(known, len(beside))

    for load in small:
        load.wait()
    for load in loads[1:] + [last]:
        load.start()
    for i in range(4):
        row = kept[pl.ds(i * 128, 128)].reshape(1, 128)
        column[i * 128:(i + 1) * 128, :] = jnp.broadcast_to(row, (128, 128)).T
    lane = lax.broadcasted_iota(jnp.int32, (32, 128), 1)
    marks = [signs[pl.ds(j * 128, 128)].reshape(1, 128).astype(jnp.float32) for j in range(width // 128)]

    def sign_of(bits):
        return (1 - 2 * (lax.population_count(bits) & 1)).astype(jnp.float32)

    for rc in (1, 0):
        for rx in range(2):
            for rz in range(4):
                owner = (z + rz) % 4 * 4 + (x + rx) % 2 * 2 + (core + rc) % 2
                index = column[pl.ds(pl.multiple_of(owner * 32, 32), 32), :]
                low = sign_of(index & (lane + place * width))
                flips = [(1 - 2 * (index >> b & 1)).astype(jnp.float32) for b in (7, 8, 9)]
                halves = [(rc * 2 + rx) * 128 + PIECES.index((rz, half)) * 16 for half in range(2)]
                for j in range(width // 128):
                    value = low * marks[j]
                    for b in range(3):
                        if j >> b & 1:
                            value = value * flips[b]
                    value = value.astype(jnp.bfloat16)
                    for half in range(2):
                        hada[halves[half]:halves[half] + 16, j * 128:(j + 1) * 128] = value[half * 16:half * 16 + 16]

    def start(src, dst, recv, peer):
        transfer(src, dst, send_sem, recv, peer).start()

    def arrived(dst, recv):
        transfer(dst, dst, send_sem, recv, sibling).wait_recv()

    def lines(i):
        return slice(0, 2) if CHUNKS[i][0] == "B" else slice(0, 1)

    def matmul(group):
        first, count = GROUPS[group]
        size = sum(CHUNKS[i][1] for i in range(first, first + count))
        loads[group].wait()
        value = lax.dot_general(
            hada[...], pixels[pl.ds(STARTS[first], size), :], (((1,), (1,)), ((), ())), preferred_element_type=jnp.float32
        )
        for i in range(first, first + count):
            at = STARTS[i] - STARTS[first]
            part[i][...] = value[:, at:at + CHUNKS[i][1]].reshape(part[i].shape)
        if first == 0:
            pl.semaphore_wait(barrier, len(greeted))
        for i in range(first, first + count):
            start(part[i].at[1], fromcore[i], own_sem.at[i], sibling)

    def first_round(i):
        rx = lines(i)
        if CHUNKS[i][0] == "D":
            start(part[i].at[0, 0, 2:4], z_first[i].at[2, 0], first_sem.at[i], opposite)
            start(part[i].at[0, 0, 0:2], z_first[i].at[0, 0], first_sem.at[i], above)
            start(part[i].at[0, 0, 4:6], z_first[i].at[1, 0], first_sem.at[i], below)
        else:
            start(part[i].at[0, rx, 1:3], z_first[i].at[0], first_sem.at[i], above)
            start(part[i].at[0, rx, 3:5], z_first[i].at[1], first_sem.at[i], below)

    def core_done(i):
        arrived(fromcore[i], own_sem.at[i])
        if CHUNKS[i][0] == "B":
            part[i][0, :, 1:5] = part[i][0, :, 1:5] + fromcore[i][:, 1:5]
            first_round(i)
            part[i][0, :, 0:1] = part[i][0, :, 0:1] + fromcore[i][:, 0:1]
            part[i][0, :, 5:8] = part[i][0, :, 5:8] + fromcore[i][:, 5:8]
        else:
            part[i][0, 1] = part[i][0, 1] + fromcore[i][1]
            start(part[i].at[0, 1], fromx[i], x_sem.at[i], across)
            part[i][0, 0] = part[i][0, 0] + fromcore[i][0]

    def x_done(i):
        arrived(fromx[i], x_sem.at[i])
        part[i][0, 0, 0:6] = part[i][0, 0, 0:6] + fromx[i][0:6]
        first_round(i)
        part[i][0, 0, 6:8] = part[i][0, 0, 6:8] + fromx[i][6:8]

    def first_done(i):
        rx = lines(i)
        arrived(z_first[i], first_sem.at[i])
        part[i][0, rx, 0] = part[i][0, rx, 0] + z_first[i][0, :, 1]
        start(part[i].at[0, rx, 0], z_second[i].at[0], own_sem.at[i], above)
        part[i][0, rx, 5] = part[i][0, rx, 5] + z_first[i][1, :, 0]
        start(part[i].at[0, rx, 5], z_second[i].at[1], own_sem.at[i], below)

    def ring_sum(i, rx):
        upper = part[i][0, rx, 6] + z_first[i][1, rx, 1] + z_second[i][0, rx]
        lower = part[i][0, rx, 7] + z_first[i][0, rx, 0] + z_second[i][1, rx]
        return upper, lower

    def second_done(i):
        if CHUNKS[i][0] == "D":
            arrived(z_first[i], first_sem.at[i])
            both = part[i][0, 0, 6:8] + z_first[i][0, 0] + z_first[i][1, 0] + z_first[i][2, 0]
            finish(i, (both[0], both[1]))
            return
        arrived(z_second[i], own_sem.at[i])
        if CHUNKS[i][0] == "A":
            finish(i, ring_sum(i, 0))
        else:
            upper, lower = ring_sum(i, 1)
            part[i][0, 1, 6] = upper
            part[i][0, 1, 7] = lower
            start(part[i].at[0, 1, 6:8], fromx[i], x_sem.at[i], across)
            upper, lower = ring_sum(i, 0)
            part[i][0, 0, 6] = upper
            part[i][0, 0, 7] = lower

    def late_done(i):
        arrived(fromx[i], x_sem.at[i])
        finish(i, (part[i][0, 0, 6] + fromx[i][0], part[i][0, 0, 7] + fromx[i][1]))

    finished = []

    def finish(i, halves):
        picked = jnp.concatenate(halves, axis=0) * float(NPIX) ** (-0.5)
        robust = picked * lax.rsqrt(1.0 + picked * picked)
        high = robust.astype(jnp.bfloat16)
        rest = (robust - high.astype(jnp.float32)).astype(jnp.bfloat16)
        both = jnp.concatenate([high, rest], axis=0)
        if not finished:
            last.wait()
        term = jnp.dot(both, weights[pl.ds(STARTS[i], CHUNKS[i][1]), :], preferred_element_type=jnp.float32)
        term = term[:32] + term[32:]
        for n in range(2):
            fresh = term[:, n * 128:(n + 1) * 128]
            total[n] = total[n] + fresh if finished else fresh
        finished.append(i)

    steps = dict(m=matmul, c=core_done, x=x_done, f=first_done, s=second_done, l=late_done)
    for at, (name, i) in enumerate(ORDER):
        steps[name](i)
        if at == len(ORDER) // 4:
            tell(near)
        if at == len(ORDER) // 2:
            hear(near)
            tell(far)
    hear(far)

    for n in range(8):
        lanes = slice(n % 4 * 32, n % 4 * 32 + 32)
        packed[n] = jnp.concatenate([total[n // 4, 8 * q:8 * q + 8, lanes] for q in range(4)], axis=1)
    for step, peer in enumerate(others):
        transfer(packed.at[peer["img"]], slabs.at[step], slab_send, slab_recv, peer).start()
    sent = pixels.at[pl.ds(0, 480 * 4 * pixels.shape[0] // (2 * width))]
    transfer(sent, sent, send_sem, slab_recv, sibling).wait_send()
    transfer(slabs, slabs, slab_send, slab_recv, sibling).wait_recv()
    result = packed[slab]
    for step in range(len(others)):
        result = result + slabs[step]
    block = jnp.concatenate([result[:, 32 * q:32 * q + 32] for q in range(4)], axis=0)
    out[...] = block.T
    transfer(slabs, slabs, slab_send, slab_recv, sibling).wait_send()


def local(images, signs, kept, omega):
    rows, width = images.shape
    scratch = [
        pltpu.VMEM(signs.shape, jnp.int32),
        pltpu.VMEM(kept.shape, jnp.int32),
        pltpu.VMEM((rows, width), jnp.bfloat16),
        pltpu.VMEM(omega.shape, jnp.bfloat16),
        pltpu.VMEM((512, width), jnp.bfloat16),
        pltpu.VMEM((512, 128), jnp.int32),
        pltpu.VMEM((2, 32, 128), jnp.float32),
        pltpu.VMEM((8, 8, 128), jnp.float32),
        pltpu.VMEM((7, 8, 128), jnp.float32),
        pltpu.SemaphoreType.DMA((len(GROUPS),)),
        pltpu.SemaphoreType.DMA((2,)),
        pltpu.SemaphoreType.DMA,
        pltpu.SemaphoreType.DMA((COUNT,)),
        pltpu.SemaphoreType.DMA((COUNT,)),
        pltpu.SemaphoreType.DMA((COUNT,)),
        pltpu.SemaphoreType.DMA,
        pltpu.SemaphoreType.DMA,
        pltpu.SemaphoreType.REGULAR,
        pltpu.SemaphoreType.REGULAR,
    ]
    lines = [2 if kind == "B" else 1 for kind, _ in CHUNKS]
    scratch += [pltpu.VMEM((2, 2, 8, 16, size), jnp.float32) for _, size in CHUNKS]
    scratch += [pltpu.VMEM((2, 8, 16, size), jnp.float32) for _, size in CHUNKS]
    scratch += [pltpu.VMEM((2 if kind == "B" else 8, 16, size), jnp.float32) for kind, size in CHUNKS]
    scratch += [pltpu.VMEM((3 if kind == "D" else 2, n, 2, 16, size), jnp.float32) for n, (kind, size) in zip(lines, CHUNKS)]
    scratch += [pltpu.VMEM((2, n, 16, size), jnp.float32) for n, (_, size) in zip(lines, CHUNKS)]
    return pl.pallas_call(
        kernel,
        out_shape=jax.ShapeDtypeStruct((32, 32), jnp.float32),
        in_specs=[pl.BlockSpec(memory_space=pl.ANY)] * 4,
        out_specs=pl.BlockSpec(memory_space=pltpu.VMEM),
        scratch_shapes=scratch,
        compiler_params=pltpu.CompilerParams(collective_id=0, has_side_effects=True, vmem_limit_bytes=48 << 20),
        cost_estimate=pl.CostEstimate(flops=2 * rows * width * 512, bytes_accessed=5 << 20, transcendentals=0),
        name="sketch",
    )(*(pltpu.with_memory_space_constraint(array, pltpu.HBM) for array in (images, signs, kept, omega)))


def solution(mesh):
    in_specs = (P("img", "pix"), P("pix"), P(), P("img", None))
    out_specs = P("img", "pix")
    return jax.shard_map(local, mesh=mesh, in_specs=in_specs, out_specs=out_specs, check_vma=False)
```

```python
import functools

import jax
import jax.numpy as jnp
from jax import lax
from jax.experimental import pallas as pl
from jax.experimental.pallas import tpu as pltpu
from jax.sharding import PartitionSpec as P

NPIX = 16384
MESH = pl.DeviceIdType.MESH
CHUNKS = (
    ("B", 256), ("A", 256), ("B", 256), ("A", 256), ("B", 256), ("B", 256), ("B", 128), ("D", 256), ("D", 128),
)
COUNT = len(CHUNKS)
STARTS = [sum(size for _, size in CHUNKS[:i]) for i in range(COUNT)]
GROUPS = ((0, 2), (2, 2), (4, 2), (6, 3))
ORDER = (
    ("m", 0), ("m", 1), ("c", 0), ("c", 1), ("m", 2), ("c", 2), ("c", 3), ("m", 3), ("c", 4), ("c", 5),
    ("c", 6), ("c", 7), ("c", 8), ("f", 0), ("x", 1), ("f", 2), ("f", 4), ("x", 3), ("f", 5), ("f", 6),
    ("s", 0), ("f", 1), ("x", 7), ("s", 2), ("s", 4), ("x", 8), ("f", 3), ("l", 0), ("s", 5), ("s", 6),
    ("s", 1), ("l", 2), ("l", 4), ("s", 7), ("l", 5), ("s", 3), ("s", 8), ("l", 6),
)
PIECES = ((1, 0), (1, 1), (2, 0), (2, 1), (3, 0), (3, 1), (0, 0), (0, 1))


def transfer(src, dst, send, recv, peer):
    return pltpu.make_async_remote_copy(
        src_ref=src, dst_ref=dst, send_sem=send, recv_sem=recv, device_id=peer, device_id_type=MESH
    )


def kernel(images, signs_far, kept_far, omega, out, signs, kept, pixels, weights, hada, column, total, packed, slabs,
           load_sem, small_sem, send_sem, own_sem, x_sem, first_sem, slab_send, slab_recv, near, far, *buffers):
    part, fromcore, fromx, z_first, z_second = (buffers[n * COUNT:(n + 1) * COUNT] for n in range(5))
    place, slab = lax.axis_index("pix"), lax.axis_index("img")
    width = images.shape[1]
    z, x, core = place // 4, place // 2 % 2, place % 2
    sibling = {"pix": z * 4 + x * 2 + (1 - core)}
    across = {"pix": z * 4 + (1 - x) * 2 + core}
    above = {"pix": (z + 1) % 4 * 4 + x * 2 + core}
    below = {"pix": (z + 3) % 4 * 4 + x * 2 + core}
    opposite = {"pix": (z + 2) % 4 * 4 + x * 2 + core}
    others = [{"img": (slab + step) % 8} for step in range(1, 8)]

    loads = []
    for group, (first, count) in enumerate(GROUPS):
        here = pl.ds(STARTS[first], sum(CHUNKS[i][1] for i in range(first, first + count)))
        loads.append(pltpu.make_async_copy(images.at[here], pixels.at[here], load_sem.at[group]))
    small = [
        pltpu.make_async_copy(kept_far, kept, small_sem.at[0]),
        pltpu.make_async_copy(signs_far, signs, small_sem.at[1]),
    ]
    last = pltpu.make_async_copy(omega, weights, small_sem.at[0])
    for load in small + loads[:1]:
        load.start()
    barrier = pltpu.get_barrier_semaphore()
    beside = [{"img": slab // 4 * 4 + (slab + step) % 4} for step in (1, 3)] + [{"img": (slab + 4) % 8}]
    greeted = [sibling, across, above, below] + beside
    for peer in greeted:
        pl.semaphore_signal(barrier, inc=1, device_id=peer, device_id_type=MESH)

    def tell(known):
        for peer in beside:
            pl.semaphore_signal(known, inc=1, device_id=peer, device_id_type=MESH)

    def hear(known):
        pl.semaphore_wait(known, len(beside))

    for load in small:
        load.wait()
    for load in loads[1:] + [last]:
        load.start()
    for i in range(4):
        row = kept[pl.ds(i * 128, 128)].reshape(1, 128)
        column[i * 128:(i + 1) * 128, :] = jnp.broadcast_to(row, (128, 128)).T
    lane = lax.broadcasted_iota(jnp.int32, (32, 128), 1)
    marks = [signs[pl.ds(j * 128, 128)].reshape(1, 128).astype(jnp.float32) for j in range(width // 128)]

    def sign_of(bits):
        return (1 - 2 * (lax.population_count(bits) & 1)).astype(jnp.float32)

    def build(rc):
        for rx in range(2):
            for rz in range(4):
                owner = (z + rz) % 4 * 4 + (x + rx) % 2 * 2 + (core + rc) % 2
                index = column[pl.ds(pl.multiple_of(owner * 32, 32), 32), :]
                low = sign_of(index & (lane + place * width))
                flips = [(1 - 2 * (index >> b & 1)).astype(jnp.float32) for b in (7, 8, 9)]
                halves = [(rc * 2 + rx) * 128 + PIECES.index((rz, half)) * 16 for half in range(2)]
                for j in range(width // 128):
                    value = low * marks[j]
                    for b in range(3):
                        if j >> b & 1:
                            value = value * flips[b]
                    value = value.astype(jnp.bfloat16)
                    for half in range(2):
                        hada[halves[half]:halves[half] + 16, j * 128:(j + 1) * 128] = value[half * 16:half * 16 + 16]

    build(1)

    def start(src, dst, recv, peer):
        transfer(src, dst, send_sem, recv, peer).start()

    def arrived(dst, recv):
        transfer(dst, dst, send_sem, recv, sibling).wait_recv()

    def lines(i):
        return slice(0, 2) if CHUNKS[i][0] == "B" else slice(0, 1)

    def matmul(group):
        first, count = GROUPS[group]
        size = sum(CHUNKS[i][1] for i in range(first, first + count))
        loads[group].wait()

        def multiply(rows):
            return lax.dot_general(
                hada[rows, :], pixels[pl.ds(STARTS[first], size), :], (((1,), (1,)), ((), ())),
                preferred_element_type=jnp.float32,
            )

        def exchange():
            for i in range(first, first + count):
                start(part[i].at[1], fromcore[i], own_sem.at[i], sibling)

        if first == 0:
            for rc in (1, 0):
                value = multiply(slice(rc * 256, rc * 256 + 256))
                for i in range(first, first + count):
                    at = STARTS[i] - STARTS[first]
                    part[i][rc] = value[:, at:at + CHUNKS[i][1]].reshape(part[i].shape[1:])
                if rc == 1:
                    pl.semaphore_wait(barrier, len(greeted))
                    exchange()
                    build(0)
            return
        value = multiply(slice(0, 512))
        for i in range(first, first + count):
            at = STARTS[i] - STARTS[first]
            part[i][...] = value[:, at:at + CHUNKS[i][1]].reshape(part[i].shape)
        exchange()

    def first_round(i):
        rx = lines(i)
        if CHUNKS[i][0] == "D":
            start(part[i].at[0, 0, 2:4], z_first[i].at[2, 0], first_sem.at[i], opposite)
            start(part[i].at[0, 0, 0:2], z_first[i].at[0, 0], first_sem.at[i], above)
            start(part[i].at[0, 0, 4:6], z_first[i].at[1, 0], first_sem.at[i], below)
        else:
            start(part[i].at[0, rx, 1:3], z_first[i].at[0], first_sem.at[i], above)
            start(part[i].at[0, rx, 3:5], z_first[i].at[1], first_sem.at[i], below)

    def core_done(i):
        arrived(fromcore[i], own_sem.at[i])
        if CHUNKS[i][0] == "B":
            part[i][0, :, 1:5] = part[i][0, :, 1:5] + fromcore[i][:, 1:5]
            first_round(i)
            part[i][0, :, 0:1] = part[i][0, :, 0:1] + fromcore[i][:, 0:1]
            part[i][0, :, 5:8] = part[i][0, :, 5:8] + fromcore[i][:, 5:8]
        else:
            part[i][0, 1] = part[i][0, 1] + fromcore[i][1]
            start(part[i].at[0, 1], fromx[i], x_sem.at[i], across)
            part[i][0, 0] = part[i][0, 0] + fromcore[i][0]

    def x_done(i):
        arrived(fromx[i], x_sem.at[i])
        part[i][0, 0, 0:6] = part[i][0, 0, 0:6] + fromx[i][0:6]
        first_round(i)
        part[i][0, 0, 6:8] = part[i][0, 0, 6:8] + fromx[i][6:8]

    def first_done(i):
        rx = lines(i)
        arrived(z_first[i], first_sem.at[i])
        part[i][0, rx, 0] = part[i][0, rx, 0] + z_first[i][0, :, 1]
        start(part[i].at[0, rx, 0], z_second[i].at[0], own_sem.at[i], above)
        part[i][0, rx, 5] = part[i][0, rx, 5] + z_first[i][1, :, 0]
        start(part[i].at[0, rx, 5], z_second[i].at[1], own_sem.at[i], below)

    def ring_sum(i, rx):
        upper = part[i][0, rx, 6] + z_first[i][1, rx, 1] + z_second[i][0, rx]
        lower = part[i][0, rx, 7] + z_first[i][0, rx, 0] + z_second[i][1, rx]
        return upper, lower

    def second_done(i):
        if CHUNKS[i][0] == "D":
            arrived(z_first[i], first_sem.at[i])
            both = part[i][0, 0, 6:8] + z_first[i][0, 0] + z_first[i][1, 0] + z_first[i][2, 0]
            finish(i, (both[0], both[1]))
            return
        arrived(z_second[i], own_sem.at[i])
        if CHUNKS[i][0] == "A":
            finish(i, ring_sum(i, 0))
        else:
            upper, lower = ring_sum(i, 1)
            part[i][0, 1, 6] = upper
            part[i][0, 1, 7] = lower
            start(part[i].at[0, 1, 6:8], fromx[i], x_sem.at[i], across)
            upper, lower = ring_sum(i, 0)
            part[i][0, 0, 6] = upper
            part[i][0, 0, 7] = lower

    def late_done(i):
        arrived(fromx[i], x_sem.at[i])
        finish(i, (part[i][0, 0, 6] + fromx[i][0], part[i][0, 0, 7] + fromx[i][1]))

    finished = []

    def finish(i, halves):
        picked = jnp.concatenate(halves, axis=0) * float(NPIX) ** (-0.5)
        robust = picked * lax.rsqrt(1.0 + picked * picked)
        high = robust.astype(jnp.bfloat16)
        rest = (robust - high.astype(jnp.float32)).astype(jnp.bfloat16)
        both = jnp.concatenate([high, rest], axis=0)
        if not finished:
            last.wait()
        term = jnp.dot(both, weights[pl.ds(STARTS[i], CHUNKS[i][1]), :], preferred_element_type=jnp.float32)
        term = term[:32] + term[32:]
        for n in range(2):
            fresh = term[:, n * 128:(n + 1) * 128]
            total[n] = total[n] + fresh if finished else fresh
        finished.append(i)

    steps = dict(m=matmul, c=core_done, x=x_done, f=first_done, s=second_done, l=late_done)
    for at, (name, i) in enumerate(ORDER):
        steps[name](i)
        if at == len(ORDER) // 4:
            tell(near)
        if at == len(ORDER) // 2:
            hear(near)
            tell(far)
    hear(far)

    for n in range(8):
        lanes = slice(n % 4 * 32, n % 4 * 32 + 32)
        packed[n] = jnp.concatenate([total[n // 4, 8 * q:8 * q + 8, lanes] for q in range(4)], axis=1)
    for step, peer in enumerate(others):
        transfer(packed.at[peer["img"]], slabs.at[step], slab_send, slab_recv, peer).start()
    sent = pixels.at[pl.ds(0, 480 * 4 * pixels.shape[0] // (2 * width))]
    transfer(sent, sent, send_sem, slab_recv, sibling).wait_send()
    transfer(slabs, slabs, slab_send, slab_recv, sibling).wait_recv()
    result = packed[slab]
    for step in range(len(others)):
        result = result + slabs[step]
    block = jnp.concatenate([result[:, 32 * q:32 * q + 32] for q in range(4)], axis=0)
    out[...] = block.T
    transfer(slabs, slabs, slab_send, slab_recv, sibling).wait_send()


def local(images, signs, kept, omega):
    rows, width = images.shape
    scratch = [
        pltpu.VMEM(signs.shape, jnp.int32),
        pltpu.VMEM(kept.shape, jnp.int32),
        pltpu.VMEM((rows, width), jnp.bfloat16),
        pltpu.VMEM(omega.shape, jnp.bfloat16),
        pltpu.VMEM((512, width), jnp.bfloat16),
        pltpu.VMEM((512, 128), jnp.int32),
        pltpu.VMEM((2, 32, 128), jnp.float32),
        pltpu.VMEM((8, 8, 128), jnp.float32),
        pltpu.VMEM((7, 8, 128), jnp.float32),
        pltpu.SemaphoreType.DMA((len(GROUPS),)),
        pltpu.SemaphoreType.DMA((2,)),
        pltpu.SemaphoreType.DMA,
        pltpu.SemaphoreType.DMA((COUNT,)),
        pltpu.SemaphoreType.DMA((COUNT,)),
        pltpu.SemaphoreType.DMA((COUNT,)),
        pltpu.SemaphoreType.DMA,
        pltpu.SemaphoreType.DMA,
        pltpu.SemaphoreType.REGULAR,
        pltpu.SemaphoreType.REGULAR,
    ]
    lines = [2 if kind == "B" else 1 for kind, _ in CHUNKS]
    scratch += [pltpu.VMEM((2, 2, 8, 16, size), jnp.float32) for _, size in CHUNKS]
    scratch += [pltpu.VMEM((2, 8, 16, size), jnp.float32) for _, size in CHUNKS]
    scratch += [pltpu.VMEM((2 if kind == "B" else 8, 16, size), jnp.float32) for kind, size in CHUNKS]
    scratch += [pltpu.VMEM((3 if kind == "D" else 2, n, 2, 16, size), jnp.float32) for n, (kind, size) in zip(lines, CHUNKS)]
    scratch += [pltpu.VMEM((2, n, 16, size), jnp.float32) for n, (_, size) in zip(lines, CHUNKS)]
    return pl.pallas_call(
        kernel,
        out_shape=jax.ShapeDtypeStruct((32, 32), jnp.float32),
        in_specs=[pl.BlockSpec(memory_space=pl.ANY)] * 4,
        out_specs=pl.BlockSpec(memory_space=pltpu.VMEM),
        scratch_shapes=scratch,
        compiler_params=pltpu.CompilerParams(collective_id=0, has_side_effects=True, vmem_limit_bytes=48 << 20),
        cost_estimate=pl.CostEstimate(flops=2 * rows * width * 512, bytes_accessed=5 << 20, transcendentals=0),
        name="sketch",
    )(*(pltpu.with_memory_space_constraint(array, pltpu.HBM) for array in (images, signs, kept, omega)))


def solution(mesh):
    in_specs = (P("img", "pix"), P("pix"), P(), P("img", None))
    out_specs = P("img", "pix")
    return jax.shard_map(local, mesh=mesh, in_specs=in_specs, out_specs=out_specs, check_vma=False)
```

```python
import functools

import jax
import jax.numpy as jnp
from jax import lax
from jax.experimental import pallas as pl
from jax.experimental.pallas import tpu as pltpu
from jax.sharding import PartitionSpec as P

NPIX = 16384
MESH = pl.DeviceIdType.MESH
CHUNKS = (
    ("B", 256), ("A", 256), ("B", 256), ("A", 256), ("B", 256), ("B", 256), ("B", 128), ("D", 256), ("D", 128),
)
COUNT = len(CHUNKS)
STARTS = [sum(size for _, size in CHUNKS[:i]) for i in range(COUNT)]
GROUPS = ((0, 2), (2, 2), (4, 2), (6, 3))
ORDER = (
    ("m", 0), ("m", 1), ("c", 0), ("c", 1), ("m", 2), ("c", 2), ("c", 3), ("m", 3), ("c", 4), ("c", 5),
    ("c", 6), ("c", 7), ("c", 8), ("f", 0), ("x", 1), ("f", 2), ("f", 4), ("x", 3), ("f", 5), ("f", 6),
    ("s", 0), ("f", 1), ("x", 7), ("s", 2), ("s", 4), ("x", 8), ("f", 3), ("l", 0), ("s", 5), ("s", 6),
    ("s", 1), ("l", 2), ("l", 4), ("s", 7), ("l", 5), ("s", 3), ("s", 8), ("l", 6),
)
PIECES = ((1, 0), (1, 1), (2, 0), (2, 1), (3, 0), (3, 1), (0, 0), (0, 1))


def transfer(src, dst, send, recv, peer):
    return pltpu.make_async_remote_copy(
        src_ref=src, dst_ref=dst, send_sem=send, recv_sem=recv, device_id=peer, device_id_type=MESH
    )


def kernel(images, signs_far, kept_far, omega, out, signs, kept, pixels, weights, hada, column, total, packed, slabs,
           load_sem, small_sem, send_sem, own_sem, x_sem, first_sem, slab_send, slab_recv, near, far, *buffers):
    part, fromcore, fromx, z_first, z_second = (buffers[n * COUNT:(n + 1) * COUNT] for n in range(5))
    place, slab = lax.axis_index("pix"), lax.axis_index("img")
    width = images.shape[1]
    z, x, core = place // 4, place // 2 % 2, place % 2
    sibling = {"pix": z * 4 + x * 2 + (1 - core)}
    across = {"pix": z * 4 + (1 - x) * 2 + core}
    above = {"pix": (z + 1) % 4 * 4 + x * 2 + core}
    below = {"pix": (z + 3) % 4 * 4 + x * 2 + core}
    opposite = {"pix": (z + 2) % 4 * 4 + x * 2 + core}
    others = [
        {"img": (slab // 4 + half) % 2 * 4 + (slab + step) % 4}
        for half, step in ((1, 2), (1, 1), (1, 3), (0, 2), (1, 0), (0, 1), (0, 3))
    ]

    loads = []
    for group, (first, count) in enumerate(GROUPS):
        here = pl.ds(STARTS[first], sum(CHUNKS[i][1] for i in range(first, first + count)))
        loads.append(pltpu.make_async_copy(images.at[here], pixels.at[here], load_sem.at[group]))
    small = [
        pltpu.make_async_copy(kept_far, kept, small_sem.at[0]),
        pltpu.make_async_copy(signs_far, signs, small_sem.at[1]),
    ]
    last = pltpu.make_async_copy(omega, weights, small_sem.at[0])
    for load in small + loads[:1]:
        load.start()
    barrier = pltpu.get_barrier_semaphore()
    beside = [{"img": slab // 4 * 4 + (slab + step) % 4} for step in (1, 3)] + [{"img": (slab + 4) % 8}]
    greeted = [sibling, across, above, below] + beside
    for peer in greeted:
        pl.semaphore_signal(barrier, inc=1, device_id=peer, device_id_type=MESH)

    def tell(known):
        for peer in beside:
            pl.semaphore_signal(known, inc=1, device_id=peer, device_id_type=MESH)

    def hear(known):
        pl.semaphore_wait(known, len(beside))

    for load in small:
        load.wait()
    for load in loads[1:] + [last]:
        load.start()
    for i in range(4):
        row = kept[pl.ds(i * 128, 128)].reshape(1, 128)
        column[i * 128:(i + 1) * 128, :] = jnp.broadcast_to(row, (128, 128)).T
    lane = lax.broadcasted_iota(jnp.int32, (32, 128), 1)
    marks = [signs[pl.ds(j * 128, 128)].reshape(1, 128).astype(jnp.float32) for j in range(width // 128)]

    def sign_of(bits):
        return (1 - 2 * (lax.population_count(bits) & 1)).astype(jnp.float32)

    def build(rc):
        for rx in range(2):
            for rz in range(4):
                owner = (z + rz) % 4 * 4 + (x + rx) % 2 * 2 + (core + rc) % 2
                index = column[pl.ds(pl.multiple_of(owner * 32, 32), 32), :]
                low = sign_of(index & (lane + place * width))
                flips = [(1 - 2 * (index >> b & 1)).astype(jnp.float32) for b in (7, 8, 9)]
                halves = [(rc * 2 + rx) * 128 + PIECES.index((rz, half)) * 16 for half in range(2)]
                for j in range(width // 128):
                    value = low * marks[j]
                    for b in range(3):
                        if j >> b & 1:
                            value = value * flips[b]
                    value = value.astype(jnp.bfloat16)
                    for half in range(2):
                        hada[halves[half]:halves[half] + 16, j * 128:(j + 1) * 128] = value[half * 16:half * 16 + 16]

    build(1)

    def start(src, dst, recv, peer):
        transfer(src, dst, send_sem, recv, peer).start()

    def arrived(dst, recv):
        transfer(dst, dst, send_sem, recv, sibling).wait_recv()

    def lines(i):
        return slice(0, 2) if CHUNKS[i][0] == "B" else slice(0, 1)

    def matmul(group):
        first, count = GROUPS[group]
        size = sum(CHUNKS[i][1] for i in range(first, first + count))
        loads[group].wait()

        def multiply(rows):
            return lax.dot_general(
                hada[rows, :], pixels[pl.ds(STARTS[first], size), :], (((1,), (1,)), ((), ())),
                preferred_element_type=jnp.float32,
            )

        def exchange():
            for i in range(first, first + count):
                start(part[i].at[1], fromcore[i], own_sem.at[i], sibling)

        if first == 0:
            for rc in (1, 0):
                value = multiply(slice(rc * 256, rc * 256 + 256))
                for i in range(first, first + count):
                    at = STARTS[i] - STARTS[first]
                    part[i][rc] = value[:, at:at + CHUNKS[i][1]].reshape(part[i].shape[1:])
                if rc == 1:
                    pl.semaphore_wait(barrier, len(greeted))
                    exchange()
                    build(0)
            return
        value = multiply(slice(0, 512))
        for i in range(first, first + count):
            at = STARTS[i] - STARTS[first]
            part[i][...] = value[:, at:at + CHUNKS[i][1]].reshape(part[i].shape)
        exchange()

    def first_round(i):
        rx = lines(i)
        if CHUNKS[i][0] == "D":
            start(part[i].at[0, 0, 2:4], z_first[i].at[2, 0], first_sem.at[i], opposite)
            start(part[i].at[0, 0, 0:2], z_first[i].at[0, 0], first_sem.at[i], above)
            start(part[i].at[0, 0, 4:6], z_first[i].at[1, 0], first_sem.at[i], below)
        else:
            start(part[i].at[0, rx, 1:3], z_first[i].at[0], first_sem.at[i], above)
            start(part[i].at[0, rx, 3:5], z_first[i].at[1], first_sem.at[i], below)

    def core_done(i):
        arrived(fromcore[i], own_sem.at[i])
        if CHUNKS[i][0] == "B":
            part[i][0, :, 1:5] = part[i][0, :, 1:5] + fromcore[i][:, 1:5]
            first_round(i)
            part[i][0, :, 0:1] = part[i][0, :, 0:1] + fromcore[i][:, 0:1]
            part[i][0, :, 5:8] = part[i][0, :, 5:8] + fromcore[i][:, 5:8]
        else:
            part[i][0, 1] = part[i][0, 1] + fromcore[i][1]
            start(part[i].at[0, 1], fromx[i], x_sem.at[i], across)
            part[i][0, 0] = part[i][0, 0] + fromcore[i][0]

    def x_done(i):
        arrived(fromx[i], x_sem.at[i])
        part[i][0, 0, 0:6] = part[i][0, 0, 0:6] + fromx[i][0:6]
        first_round(i)
        part[i][0, 0, 6:8] = part[i][0, 0, 6:8] + fromx[i][6:8]

    def first_done(i):
        rx = lines(i)
        arrived(z_first[i], first_sem.at[i])
        part[i][0, rx, 0] = part[i][0, rx, 0] + z_first[i][0, :, 1]
        start(part[i].at[0, rx, 0], z_second[i].at[0], own_sem.at[i], above)
        part[i][0, rx, 5] = part[i][0, rx, 5] + z_first[i][1, :, 0]
        start(part[i].at[0, rx, 5], z_second[i].at[1], own_sem.at[i], below)

    def ring_sum(i, rx):
        upper = part[i][0, rx, 6] + z_first[i][1, rx, 1] + z_second[i][0, rx]
        lower = part[i][0, rx, 7] + z_first[i][0, rx, 0] + z_second[i][1, rx]
        return upper, lower

    def second_done(i):
        if CHUNKS[i][0] == "D":
            arrived(z_first[i], first_sem.at[i])
            both = part[i][0, 0, 6:8] + z_first[i][0, 0] + z_first[i][1, 0] + z_first[i][2, 0]
            finish(i, (both[0], both[1]))
            return
        arrived(z_second[i], own_sem.at[i])
        if CHUNKS[i][0] == "A":
            finish(i, ring_sum(i, 0))
        else:
            upper, lower = ring_sum(i, 1)
            part[i][0, 1, 6] = upper
            part[i][0, 1, 7] = lower
            start(part[i].at[0, 1, 6:8], fromx[i], x_sem.at[i], across)
            upper, lower = ring_sum(i, 0)
            part[i][0, 0, 6] = upper
            part[i][0, 0, 7] = lower

    def late_done(i):
        arrived(fromx[i], x_sem.at[i])
        finish(i, (part[i][0, 0, 6] + fromx[i][0], part[i][0, 0, 7] + fromx[i][1]))

    finished = []

    def finish(i, halves):
        picked = jnp.concatenate(halves, axis=0) * float(NPIX) ** (-0.5)
        robust = picked * lax.rsqrt(1.0 + picked * picked)
        high = robust.astype(jnp.bfloat16)
        rest = (robust - high.astype(jnp.float32)).astype(jnp.bfloat16)
        both = jnp.concatenate([high, rest], axis=0)
        if not finished:
            last.wait()
        term = jnp.dot(both, weights[pl.ds(STARTS[i], CHUNKS[i][1]), :], preferred_element_type=jnp.float32)
        term = term[:32] + term[32:]
        for n in range(2):
            fresh = term[:, n * 128:(n + 1) * 128]
            total[n] = total[n] + fresh if finished else fresh
        finished.append(i)

    steps = dict(m=matmul, c=core_done, x=x_done, f=first_done, s=second_done, l=late_done)
    for at, (name, i) in enumerate(ORDER):
        steps[name](i)
        if at == len(ORDER) // 4:
            tell(near)
        if at == len(ORDER) // 2:
            hear(near)
            tell(far)
    hear(far)

    for n in range(8):
        lanes = slice(n % 4 * 32, n % 4 * 32 + 32)
        packed[n] = jnp.concatenate([total[n // 4, 8 * q:8 * q + 8, lanes] for q in range(4)], axis=1)
    for step, peer in enumerate(others):
        transfer(packed.at[peer["img"]], slabs.at[step], slab_send, slab_recv, peer).start()
    sent = pixels.at[pl.ds(0, 480 * 4 * pixels.shape[0] // (2 * width))]
    transfer(sent, sent, send_sem, slab_recv, sibling).wait_send()
    transfer(slabs, slabs, slab_send, slab_recv, sibling).wait_recv()
    result = packed[slab]
    for step in range(len(others)):
        result = result + slabs[step]
    block = jnp.concatenate([result[:, 32 * q:32 * q + 32] for q in range(4)], axis=0)
    out[...] = block.T
    transfer(slabs, slabs, slab_send, slab_recv, sibling).wait_send()


def local(images, signs, kept, omega):
    rows, width = images.shape
    scratch = [
        pltpu.VMEM(signs.shape, jnp.int32),
        pltpu.VMEM(kept.shape, jnp.int32),
        pltpu.VMEM((rows, width), jnp.bfloat16),
        pltpu.VMEM(omega.shape, jnp.bfloat16),
        pltpu.VMEM((512, width), jnp.bfloat16),
        pltpu.VMEM((512, 128), jnp.int32),
        pltpu.VMEM((2, 32, 128), jnp.float32),
        pltpu.VMEM((8, 8, 128), jnp.float32),
        pltpu.VMEM((7, 8, 128), jnp.float32),
        pltpu.SemaphoreType.DMA((len(GROUPS),)),
        pltpu.SemaphoreType.DMA((2,)),
        pltpu.SemaphoreType.DMA,
        pltpu.SemaphoreType.DMA((COUNT,)),
        pltpu.SemaphoreType.DMA((COUNT,)),
        pltpu.SemaphoreType.DMA((COUNT,)),
        pltpu.SemaphoreType.DMA,
        pltpu.SemaphoreType.DMA,
        pltpu.SemaphoreType.REGULAR,
        pltpu.SemaphoreType.REGULAR,
    ]
    lines = [2 if kind == "B" else 1 for kind, _ in CHUNKS]
    scratch += [pltpu.VMEM((2, 2, 8, 16, size), jnp.float32) for _, size in CHUNKS]
    scratch += [pltpu.VMEM((2, 8, 16, size), jnp.float32) for _, size in CHUNKS]
    scratch += [pltpu.VMEM((2 if kind == "B" else 8, 16, size), jnp.float32) for kind, size in CHUNKS]
    scratch += [pltpu.VMEM((3 if kind == "D" else 2, n, 2, 16, size), jnp.float32) for n, (kind, size) in zip(lines, CHUNKS)]
    scratch += [pltpu.VMEM((2, n, 16, size), jnp.float32) for n, (_, size) in zip(lines, CHUNKS)]
    return pl.pallas_call(
        kernel,
        out_shape=jax.ShapeDtypeStruct((32, 32), jnp.float32),
        in_specs=[pl.BlockSpec(memory_space=pl.ANY)] * 4,
        out_specs=pl.BlockSpec(memory_space=pltpu.VMEM),
        scratch_shapes=scratch,
        compiler_params=pltpu.CompilerParams(collective_id=0, has_side_effects=True, vmem_limit_bytes=48 << 20),
        cost_estimate=pl.CostEstimate(flops=2 * rows * width * 512, bytes_accessed=5 << 20, transcendentals=0),
        name="sketch",
    )(*(pltpu.with_memory_space_constraint(array, pltpu.HBM) for array in (images, signs, kept, omega)))


def solution(mesh):
    in_specs = (P("img", "pix"), P("pix"), P(), P("img", None))
    out_specs = P("img", "pix")
    return jax.shard_map(local, mesh=mesh, in_specs=in_specs, out_specs=out_specs, check_vma=False)
```

```python
import functools

import jax
import jax.numpy as jnp
from jax import lax
from jax.experimental import pallas as pl
from jax.experimental.pallas import tpu as pltpu
from jax.sharding import PartitionSpec as P

NPIX = 16384
MESH = pl.DeviceIdType.MESH
CHUNKS = (
    ("B", 256), ("A", 256), ("B", 256), ("A", 256), ("B", 256), ("D", 256), ("B", 256), ("B", 128), ("D", 128),
)
COUNT = len(CHUNKS)
STARTS = [sum(size for _, size in CHUNKS[:i]) for i in range(COUNT)]
GROUPS = ((0, 2), (2, 2), (4, 2), (6, 3))
ORDER = (
    ("m", 0), ("m", 1), ("c", 0), ("c", 1), ("m", 2), ("c", 2), ("c", 3), ("m", 3), ("c", 4), ("c", 5),
    ("c", 6), ("c", 7), ("c", 8), ("f", 0), ("x", 1), ("f", 2), ("f", 4), ("x", 3), ("f", 6), ("f", 7),
    ("s", 0), ("f", 1), ("x", 5), ("s", 2), ("s", 4), ("x", 8), ("f", 3), ("l", 0), ("s", 6), ("s", 7),
    ("s", 1), ("l", 2), ("l", 4), ("s", 5), ("l", 6), ("s", 3), ("s", 8), ("l", 7),
)
PIECES = ((1, 0), (1, 1), (2, 0), (2, 1), (3, 0), (3, 1), (0, 0), (0, 1))


def transfer(src, dst, send, recv, peer):
    return pltpu.make_async_remote_copy(
        src_ref=src, dst_ref=dst, send_sem=send, recv_sem=recv, device_id=peer, device_id_type=MESH
    )


def kernel(images, signs_far, kept_far, omega, out, signs, kept, pixels, weights, hada, column, total, packed, slabs,
           load_sem, small_sem, send_sem, own_sem, x_sem, first_sem, slab_send, slab_recv, near, far, *buffers):
    part, fromcore, fromx, z_first, z_second = (buffers[n * COUNT:(n + 1) * COUNT] for n in range(5))
    place, slab = lax.axis_index("pix"), lax.axis_index("img")
    width = images.shape[1]
    z, x, core = place // 4, place // 2 % 2, place % 2
    sibling = {"pix": z * 4 + x * 2 + (1 - core)}
    across = {"pix": z * 4 + (1 - x) * 2 + core}
    above = {"pix": (z + 1) % 4 * 4 + x * 2 + core}
    below = {"pix": (z + 3) % 4 * 4 + x * 2 + core}
    opposite = {"pix": (z + 2) % 4 * 4 + x * 2 + core}
    others = [
        {"img": (slab // 4 + half) % 2 * 4 + (slab + step) % 4}
        for half, step in ((1, 2), (1, 1), (1, 3), (0, 2), (1, 0), (0, 1), (0, 3))
    ]

    loads = []
    for group, (first, count) in enumerate(GROUPS):
        here = pl.ds(STARTS[first], sum(CHUNKS[i][1] for i in range(first, first + count)))
        loads.append(pltpu.make_async_copy(images.at[here], pixels.at[here], load_sem.at[group]))
    small = [
        pltpu.make_async_copy(kept_far, kept, small_sem.at[0]),
        pltpu.make_async_copy(signs_far, signs, small_sem.at[1]),
    ]
    last = pltpu.make_async_copy(omega, weights, small_sem.at[0])
    for load in small + loads[:1]:
        load.start()
    barrier = pltpu.get_barrier_semaphore()
    beside = [{"img": slab // 4 * 4 + (slab + step) % 4} for step in (1, 3)] + [{"img": (slab + 4) % 8}]
    greeted = [sibling, across, above, below] + beside
    for peer in greeted:
        pl.semaphore_signal(barrier, inc=1, device_id=peer, device_id_type=MESH)

    def tell(known):
        for peer in beside:
            pl.semaphore_signal(known, inc=1, device_id=peer, device_id_type=MESH)

    def hear(known):
        pl.semaphore_wait(known, len(beside))

    for load in small:
        load.wait()
    for load in loads[1:] + [last]:
        load.start()
    for i in range(4):
        row = kept[pl.ds(i * 128, 128)].reshape(1, 128)
        column[i * 128:(i + 1) * 128, :] = jnp.broadcast_to(row, (128, 128)).T
    lane = lax.broadcasted_iota(jnp.int32, (32, 128), 1)
    marks = [signs[pl.ds(j * 128, 128)].reshape(1, 128).astype(jnp.float32) for j in range(width // 128)]

    def sign_of(bits):
        return (1 - 2 * (lax.population_count(bits) & 1)).astype(jnp.float32)

    def build(rc):
        for rx in range(2):
            for rz in range(4):
                owner = (z + rz) % 4 * 4 + (x + rx) % 2 * 2 + (core + rc) % 2
                index = column[pl.ds(pl.multiple_of(owner * 32, 32), 32), :]
                low = sign_of(index & (lane + place * width))
                flips = [(1 - 2 * (index >> b & 1)).astype(jnp.float32) for b in (7, 8, 9)]
                halves = [(rc * 2 + rx) * 128 + PIECES.index((rz, half)) * 16 for half in range(2)]
                for j in range(width // 128):
                    value = low * marks[j]
                    for b in range(3):
                        if j >> b & 1:
                            value = value * flips[b]
                    value = value.astype(jnp.bfloat16)
                    for half in range(2):
                        hada[halves[half]:halves[half] + 16, j * 128:(j + 1) * 128] = value[half * 16:half * 16 + 16]

    build(1)

    def start(src, dst, recv, peer):
        transfer(src, dst, send_sem, recv, peer).start()

    def arrived(dst, recv):
        transfer(dst, dst, send_sem, recv, sibling).wait_recv()

    def lines(i):
        return slice(0, 2) if CHUNKS[i][0] == "B" else slice(0, 1)

    def matmul(group):
        first, count = GROUPS[group]
        size = sum(CHUNKS[i][1] for i in range(first, first + count))
        loads[group].wait()

        def multiply(rows):
            return lax.dot_general(
                hada[rows, :], pixels[pl.ds(STARTS[first], size), :], (((1,), (1,)), ((), ())),
                preferred_element_type=jnp.float32,
            )

        def exchange():
            for i in range(first, first + count):
                start(part[i].at[1], fromcore[i], own_sem.at[i], sibling)

        if first == 0:
            for rc in (1, 0):
                value = multiply(slice(rc * 256, rc * 256 + 256))
                for i in range(first, first + count):
                    at = STARTS[i] - STARTS[first]
                    part[i][rc] = value[:, at:at + CHUNKS[i][1]].reshape(part[i].shape[1:])
                if rc == 1:
                    pl.semaphore_wait(barrier, len(greeted))
                    exchange()
                    build(0)
            return
        value = multiply(slice(0, 512))
        for i in range(first, first + count):
            at = STARTS[i] - STARTS[first]
            part[i][...] = value[:, at:at + CHUNKS[i][1]].reshape(part[i].shape)
        exchange()

    def first_round(i):
        rx = lines(i)
        if CHUNKS[i][0] == "D":
            start(part[i].at[0, 0, 2:4], z_first[i].at[2, 0], first_sem.at[i], opposite)
            start(part[i].at[0, 0, 0:2], z_first[i].at[0, 0], first_sem.at[i], above)
            start(part[i].at[0, 0, 4:6], z_first[i].at[1, 0], first_sem.at[i], below)
        else:
            start(part[i].at[0, rx, 1:3], z_first[i].at[0], first_sem.at[i], above)
            start(part[i].at[0, rx, 3:5], z_first[i].at[1], first_sem.at[i], below)

    def core_done(i):
        arrived(fromcore[i], own_sem.at[i])
        if CHUNKS[i][0] == "B":
            part[i][0, :, 1:5] = part[i][0, :, 1:5] + fromcore[i][:, 1:5]
            first_round(i)
            part[i][0, :, 0:1] = part[i][0, :, 0:1] + fromcore[i][:, 0:1]
            part[i][0, :, 5:8] = part[i][0, :, 5:8] + fromcore[i][:, 5:8]
        else:
            part[i][0, 1] = part[i][0, 1] + fromcore[i][1]
            start(part[i].at[0, 1], fromx[i], x_sem.at[i], across)
            part[i][0, 0] = part[i][0, 0] + fromcore[i][0]

    def x_done(i):
        arrived(fromx[i], x_sem.at[i])
        part[i][0, 0, 0:6] = part[i][0, 0, 0:6] + fromx[i][0:6]
        first_round(i)
        part[i][0, 0, 6:8] = part[i][0, 0, 6:8] + fromx[i][6:8]

    def first_done(i):
        rx = lines(i)
        arrived(z_first[i], first_sem.at[i])
        part[i][0, rx, 0] = part[i][0, rx, 0] + z_first[i][0, :, 1]
        start(part[i].at[0, rx, 0], z_second[i].at[0], own_sem.at[i], above)
        part[i][0, rx, 5] = part[i][0, rx, 5] + z_first[i][1, :, 0]
        start(part[i].at[0, rx, 5], z_second[i].at[1], own_sem.at[i], below)

    def ring_sum(i, rx):
        upper = part[i][0, rx, 6] + z_first[i][1, rx, 1] + z_second[i][0, rx]
        lower = part[i][0, rx, 7] + z_first[i][0, rx, 0] + z_second[i][1, rx]
        return upper, lower

    def second_done(i):
        if CHUNKS[i][0] == "D":
            arrived(z_first[i], first_sem.at[i])
            both = part[i][0, 0, 6:8] + z_first[i][0, 0] + z_first[i][1, 0] + z_first[i][2, 0]
            finish(i, (both[0], both[1]))
            return
        arrived(z_second[i], own_sem.at[i])
        if CHUNKS[i][0] == "A":
            finish(i, ring_sum(i, 0))
        else:
            upper, lower = ring_sum(i, 1)
            part[i][0, 1, 6] = upper
            part[i][0, 1, 7] = lower
            start(part[i].at[0, 1, 6:8], fromx[i], x_sem.at[i], across)
            upper, lower = ring_sum(i, 0)
            part[i][0, 0, 6] = upper
            part[i][0, 0, 7] = lower

    def late_done(i):
        arrived(fromx[i], x_sem.at[i])
        finish(i, (part[i][0, 0, 6] + fromx[i][0], part[i][0, 0, 7] + fromx[i][1]))

    finished = []

    def finish(i, halves):
        picked = jnp.concatenate(halves, axis=0) * float(NPIX) ** (-0.5)
        robust = picked * lax.rsqrt(1.0 + picked * picked)
        high = robust.astype(jnp.bfloat16)
        rest = (robust - high.astype(jnp.float32)).astype(jnp.bfloat16)
        both = jnp.concatenate([high, rest], axis=0)
        if not finished:
            last.wait()
        term = jnp.dot(both, weights[pl.ds(STARTS[i], CHUNKS[i][1]), :], preferred_element_type=jnp.float32)
        term = term[:32] + term[32:]
        for n in range(2):
            fresh = term[:, n * 128:(n + 1) * 128]
            total[n] = total[n] + fresh if finished else fresh
        finished.append(i)

    steps = dict(m=matmul, c=core_done, x=x_done, f=first_done, s=second_done, l=late_done)
    for at, (name, i) in enumerate(ORDER):
        steps[name](i)
        if at == len(ORDER) // 4:
            tell(near)
        if at == len(ORDER) // 2:
            hear(near)
            tell(far)
    hear(far)

    for n in range(8):
        lanes = slice(n % 4 * 32, n % 4 * 32 + 32)
        packed[n] = jnp.concatenate([total[n // 4, 8 * q:8 * q + 8, lanes] for q in range(4)], axis=1)
    for step, peer in enumerate(others):
        transfer(packed.at[peer["img"]], slabs.at[step], slab_send, slab_recv, peer).start()
    sent = pixels.at[pl.ds(0, 480 * 4 * pixels.shape[0] // (2 * width))]
    transfer(sent, sent, send_sem, slab_recv, sibling).wait_send()
    transfer(slabs, slabs, slab_send, slab_recv, sibling).wait_recv()
    result = packed[slab]
    for step in range(len(others)):
        result = result + slabs[step]
    block = jnp.concatenate([result[:, 32 * q:32 * q + 32] for q in range(4)], axis=0)
    out[...] = block.T
    transfer(slabs, slabs, slab_send, slab_recv, sibling).wait_send()


def local(images, signs, kept, omega):
    rows, width = images.shape
    scratch = [
        pltpu.VMEM(signs.shape, jnp.int32),
        pltpu.VMEM(kept.shape, jnp.int32),
        pltpu.VMEM((rows, width), jnp.bfloat16),
        pltpu.VMEM(omega.shape, jnp.bfloat16),
        pltpu.VMEM((512, width), jnp.bfloat16),
        pltpu.VMEM((512, 128), jnp.int32),
        pltpu.VMEM((2, 32, 128), jnp.float32),
        pltpu.VMEM((8, 8, 128), jnp.float32),
        pltpu.VMEM((7, 8, 128), jnp.float32),
        pltpu.SemaphoreType.DMA((len(GROUPS),)),
        pltpu.SemaphoreType.DMA((2,)),
        pltpu.SemaphoreType.DMA,
        pltpu.SemaphoreType.DMA((COUNT,)),
        pltpu.SemaphoreType.DMA((COUNT,)),
        pltpu.SemaphoreType.DMA((COUNT,)),
        pltpu.SemaphoreType.DMA,
        pltpu.SemaphoreType.DMA,
        pltpu.SemaphoreType.REGULAR,
        pltpu.SemaphoreType.REGULAR,
    ]
    lines = [2 if kind == "B" else 1 for kind, _ in CHUNKS]
    scratch += [pltpu.VMEM((2, 2, 8, 16, size), jnp.float32) for _, size in CHUNKS]
    scratch += [pltpu.VMEM((2, 8, 16, size), jnp.float32) for _, size in CHUNKS]
    scratch += [pltpu.VMEM((2 if kind == "B" else 8, 16, size), jnp.float32) for kind, size in CHUNKS]
    scratch += [pltpu.VMEM((3 if kind == "D" else 2, n, 2, 16, size), jnp.float32) for n, (kind, size) in zip(lines, CHUNKS)]
    scratch += [pltpu.VMEM((2, n, 16, size), jnp.float32) for n, (_, size) in zip(lines, CHUNKS)]
    return pl.pallas_call(
        kernel,
        out_shape=jax.ShapeDtypeStruct((32, 32), jnp.float32),
        in_specs=[pl.BlockSpec(memory_space=pl.ANY)] * 4,
        out_specs=pl.BlockSpec(memory_space=pltpu.VMEM),
        scratch_shapes=scratch,
        compiler_params=pltpu.CompilerParams(collective_id=0, has_side_effects=True, vmem_limit_bytes=48 << 20),
        cost_estimate=pl.CostEstimate(flops=2 * rows * width * 512, bytes_accessed=5 << 20, transcendentals=0),
        name="sketch",
    )(*(pltpu.with_memory_space_constraint(array, pltpu.HBM) for array in (images, signs, kept, omega)))


def solution(mesh):
    in_specs = (P("img", "pix"), P("pix"), P(), P("img", None))
    out_specs = P("img", "pix")
    return jax.shard_map(local, mesh=mesh, in_specs=in_specs, out_specs=out_specs, check_vma=False)
```
